32 devices in a mesh: dp: 8 (over z, y), tensor: 4 (over x, core).
Axes of the slice: x: 2, y: 2, z: 4, core: 2. Of those that a mesh axis runs over, the one named last changes fastest.
Arguments:
- queries: bfloat16 [64, 6, 8192], P('dp', None, 'tensor'), may hold values from -150 to 150
- new_keys: bfloat16 [64, 6, 1024], P('dp', None, 'tensor'), may hold values from -6 to 6
- new_values: bfloat16 [64, 6, 1024], P('dp', None, 'tensor'), may hold values from -6 to 6
- key_cache: bfloat16 [64, 256, 1024], P('dp', None, 'tensor'), may hold values from -6 to 6
- value_cache: bfloat16 [64, 256, 1024], P('dp', None, 'tensor'), may hold values from -6 to 6
- cache_lengths: int32 [64], P('dp'), may hold values from 32 to 256, as said below
- accepted: int32 [64], P('tensor'), may hold values from 1 to 6
- residual: bfloat16 [64, 6, 8192], P('tensor', None, 'dp'), may hold values from -6 to 6
- out_weight: bfloat16 [8192, 8192], P('tensor', 'dp'), may hold values from -0.0625 to 0.0625
- draft_weight: bfloat16 [8192, 8192], P('tensor', 'dp'), may hold values from -0.0625 to 0.0625
Outputs:
- verified: bfloat16 [64, 6, 8192], P('tensor', None, 'dp')
- drafted: bfloat16 [5, 64, 8192], P(None, 'tensor', 'dp')
The draws below stay inside these ranges and needn't reach their ends.
Inputs may be any that keep to these rules, and one draw needn't show every extreme that they name: `cache_lengths`: every draw has a window with all 256 slots live.
All inputs are finite; a program needn't handle non-finite values.
Results may differ from the reference program's by a relative error of at most 0.008.
Values may be sent and summed in bfloat16 or wider, within the bound.
A program may use at most 64 MiB of HBM per device.

```python
import jax
import jax.numpy as jnp
from jax import lax

D = 8192
HD = 128
HEADS = 64
KVH = 8
Q = 6
STEPS = 5
CACHE = 256
WINDOWS = 64


def cache_base(key):
    return jnp.clip(jax.random.normal(jax.random.fold_in(key, 11), (WINDOWS, CACHE, KVH * HD), jnp.float32), -6.0, 6.0)


def draw_key_cache(key, part):
    base = cache_base(key)
    return base.astype(jnp.bfloat16)


def draw_queries(key, part):
    values = jnp.clip(jax.random.normal(jax.random.fold_in(key, 12), (WINDOWS, Q, HEADS * HD), jnp.float32), -6.0, 6.0)
    return values.astype(jnp.bfloat16)


def draw_cache_lengths(key, part):
    lengths = jax.random.randint(jax.random.fold_in(key, 13), (WINDOWS,), CACHE // 8, CACHE + 1, dtype=jnp.int32)
    return lengths.at[0].set(CACHE)


def place_ends(values, own_key, low, high):
    longest = values.shape.index(max(values.shape))
    spots = []
    for shift in (0, 1):
        where = [jax.random.randint(jax.random.fold_in(own_key, axis), (), 0, length) for axis, length in enumerate(values.shape)]
        where[longest] = (where[longest] + shift) % values.shape[longest]
        spots.append(tuple(where))
    return values.at[spots[0]].set(low).at[spots[1]].set(high)


def shard_levels(own_key, shape, shards, smallest, high):
    def one(position, blocks):
        steps = jax.random.uniform(jax.random.fold_in(jax.random.fold_in(own_key, 6), position), (blocks,), jnp.float32, smallest / len(shards), high / len(shards))
        return jnp.repeat(jnp.exp(steps), shape[position] // blocks).reshape((-1,) + (1,) * (len(shape) - position - 1))

    loudness = one(*shards[0])
    for cut in shards[1:]:
        loudness = loudness * one(*cut)
    return loudness


def noise(stream_key, extent, width, most, split=(), held_as=jnp.bfloat16):
    entries = jax.random.normal(stream_key, extent, jnp.float32) * width
    if len(split) > 0:
        entries = shard_levels(stream_key, extent, split, -0.22, 0.18) * entries
    return jnp.clip(entries, min=-most, max=most).astype(held_as)


def setup_inputs(seed: int = 0) -> dict:
    seeds = jax.random.split(jax.random.key(seed), 11)
    return {
        "queries": draw_queries(jax.random.fold_in(seeds[10], 71), 0),
        "new_keys": noise(seeds[1], (WINDOWS, Q, KVH * HD), 1.0, 6.0, ((0, 8), (2, 4))),
        "new_values": noise(seeds[2], (WINDOWS, Q, KVH * HD), 1.0, 6.0, ((0, 8), (2, 4))),
        "key_cache": draw_key_cache(jax.random.fold_in(seeds[10], 71), 0),
        "value_cache": noise(seeds[4], (WINDOWS, CACHE, KVH * HD), 1.0, 6.0, ((0, 8), (2, 4))),
        "cache_lengths": draw_cache_lengths(jax.random.fold_in(seeds[10], 71), 0),
        "accepted": place_ends(jax.random.randint(seeds[6], (WINDOWS,), 1, Q + 1), jax.random.fold_in(seeds[6], 1), 1, Q).astype(jnp.int32),
        "residual": noise(seeds[7], (WINDOWS, Q, D), 1.0, 6.0, ((0, 4), (2, 8))),
        "out_weight": noise(seeds[8], (HEADS * HD, D), (HEADS * HD) ** -0.5, 0.0625, ((0, 4), (1, 8))),
        "draft_weight": noise(seeds[9], (D, D), D ** -0.5, 0.0625, ((0, 4), (1, 8))),
    }


def attend_window(packed):
    query_rows, fresh_keys, fresh_values, cache_keys, cache_values, length = packed
    group_size = HEADS // KVH
    query_float = query_rows.astype(jnp.float32).reshape(Q, KVH, group_size, HD)
    keys_cached = cache_keys.astype(jnp.float32).reshape(CACHE, KVH, HD)
    keys_fresh = fresh_keys.astype(jnp.float32).reshape(Q, KVH, HD)
    score_cache = jnp.einsum("tkgd,pkd->kgtp", query_float, keys_cached) * (HD ** -0.5)
    score_fresh = jnp.einsum("tkgd,pkd->kgtp", query_float, keys_fresh) * (HD ** -0.5)
    live_cache = jnp.arange(CACHE) < length
    live_fresh = jnp.arange(Q)[None, :] <= jnp.arange(Q)[:, None]
    scores = jnp.concatenate([jnp.where(live_cache, score_cache, -jnp.inf), jnp.where(live_fresh, score_fresh, -jnp.inf)], axis=-1)
    largest = jnp.max(scores, axis=-1, keepdims=True)
    powered = jnp.exp(scores - largest)
    weights = (powered / jnp.sum(powered, axis=-1, keepdims=True)).astype(jnp.bfloat16).astype(jnp.float32)
    values_cached = cache_values.astype(jnp.float32).reshape(CACHE, KVH, HD)
    values_fresh = fresh_values.astype(jnp.float32).reshape(Q, KVH, HD)
    mixed_rows = jnp.einsum("kgtp,pkd->tkgd", weights[..., :CACHE], values_cached) + jnp.einsum("kgtp,pkd->tkgd", weights[..., CACHE:], values_fresh)
    return mixed_rows.reshape(Q, HEADS * HD).astype(jnp.bfloat16)


def reference(queries, new_keys, new_values, key_cache, value_cache, cache_lengths, accepted, residual, out_weight, draft_weight):
    attended = lax.map(attend_window, (queries, new_keys, new_values, key_cache, value_cache, cache_lengths))
    flat_rows = attended.reshape(WINDOWS * Q, HEADS * HD)
    projected = jnp.dot(flat_rows, out_weight, preferred_element_type=jnp.float32)
    verified = (residual.reshape(WINDOWS * Q, D).astype(jnp.float32) + projected).astype(jnp.bfloat16).reshape(WINDOWS, Q, D)
    feature = verified[jnp.arange(WINDOWS), accepted - 1]
    results = []
    for draft_step in range(STEPS):
        feature = jnp.tanh(2.0 * jnp.dot(feature, draft_weight, preferred_element_type=jnp.float32)).astype(jnp.bfloat16)
        results.append(feature)
    return verified, jnp.stack(results)
```

```python
import functools

import jax
import jax.numpy as jnp
from jax import lax
from jax.experimental import pallas as pl
from jax.experimental.pallas import tpu as pltpu
from jax.sharding import PartitionSpec as P

HD = 128
STEPS = 5


MESH = pl.DeviceIdType.MESH
BF16 = jnp.bfloat16
F32 = jnp.float32


def draft_kernel(
    nt,
    nd,
    picked_ref,
    weight_hbm,
    out_ref,
    weight,
    pieces,
    spread,
    feats,
    partial,
    outgoing,
    landed,
    weight_sem,
    spread_send,
    spread_recv,
    feat_send,
    feat_recv,
    part_send,
    part_recv,
):
    rows, cols = picked_ref.shape
    minors = nd // nt
    me_t = lax.axis_index("tensor")
    me_d = lax.axis_index("dp")
    group = me_d // minors
    minor = me_d % minors

    load = pltpu.make_async_copy(weight_hbm, weight, weight_sem)
    load.start()
    barrier = pltpu.get_barrier_semaphore()
    for k in range(nt):
        for j in range(minors):
            if k or j:
                peer = (group * minors + (minor + j) % minors, (me_t + k) % nt)
                pl.semaphore_signal(barrier, inc=1, device_id=peer, device_id_type=MESH)
    for i in range(1, nt):
        peer = ((group + i) % nt * minors + minor, me_t)
        pl.semaphore_signal(barrier, inc=1, device_id=peer, device_id_type=MESH)
    pieces[0] = picked_ref[...]
    pl.semaphore_wait(barrier, nt * minors - 1 + nt - 1)
    load.wait()

    def spread_copy(s, i):
        return pltpu.make_async_remote_copy(
            src_ref=pieces.at[s],
            dst_ref=spread.at[s, i - 1],
            send_sem=spread_send.at[s, i - 1],
            recv_sem=spread_recv.at[s, i - 1],
            device_id=((group + i) % nt * minors + minor, me_t),
            device_id_type=MESH,
        )

    def feat_slot(s):
        return feats.at[
            s,
            pl.ds(pl.multiple_of(me_t * rows, rows), rows),
            pl.ds(pl.multiple_of(minor * cols, cols), cols),
        ]

    def feat_copy(s, i, j):
        return pltpu.make_async_remote_copy(
            src_ref=pieces.at[s] if i == 0 else spread.at[s, i - 1],
            dst_ref=feat_slot(s),
            send_sem=feat_send.at[s, i, j],
            recv_sem=feat_recv.at[s, me_t, minor],
            device_id=(group * minors + (minor + j) % minors, (group + nt - i) % nt),
            device_id_type=MESH,
        )

    def feat_local(s, i):
        return pltpu.make_async_copy(
            pieces.at[s] if i == 0 else spread.at[s, i - 1],
            feat_slot(s),
            feat_recv.at[s, me_t, minor],
        )

    def part_copy(s, k):
        return pltpu.make_async_remote_copy(
            src_ref=outgoing.at[s, pl.ds(pl.multiple_of((me_t + k) % nt * rows, rows), rows)],
            dst_ref=landed.at[s, k - 1],
            send_sem=part_send.at[s, k - 1],
            recv_sem=part_recv.at[s, k - 1],
            device_id=(me_d, (me_t + k) % nt),
            device_id_type=MESH,
        )

    order = sorted(range(nt), key=lambda i: min(i, nt - i))

    def step(s, carry):
        for i in order[1:]:
            spread_copy(s, i).start()
        for i in order:
            if i:
                spread_copy(s, i).wait_recv()
            target = (group + nt - i) % nt
            for j in range(1, minors):
                feat_copy(s, i, j).start()

            @pl.when(target != me_t)
            def _():
                feat_copy(s, i, 0).start()

            @pl.when(target == me_t)
            def _():
                feat_local(s, i).start()

        for t in range(nt):
            for m in range(minors):
                pltpu.make_async_copy(
                    pieces.at[s],
                    feats.at[s, pl.ds(t * rows, rows), pl.ds(m * cols, cols)],
                    feat_recv.at[s, t, m],
                ).wait()
        for c in range(0, cols, 256):
            product = jnp.dot(
                feats[s], weight[:, c : c + 256], preferred_element_type=F32
            )
            partial[:, c : c + 256] = product
            outgoing[s, :, c : c + 256] = product.astype(BF16)
        for k in range(1, nt):
            part_copy(s, k).start()
        total = partial[pl.ds(pl.multiple_of(me_t * rows, rows), rows), :]
        for k in range(1, nt):
            part_copy(s, k).wait_recv()
            total = total + landed[s, k - 1].astype(F32)
        drafted = jnp.tanh(2.0 * total).astype(BF16)
        out_ref[s] = drafted
        pieces[s + 1] = drafted
        return carry

    lax.fori_loop(0, STEPS, step, 0)

    def drain(s, carry):
        for i in range(nt):
            if i:
                spread_copy(s, i).wait_send()
                part_copy(s, i).wait_send()
            for j in range(1, minors):
                feat_copy(s, i, j).wait_send()

            @pl.when((group + nt - i) % nt != me_t)
            def _():
                feat_copy(s, i, 0).wait_send()

        return carry

    lax.fori_loop(0, STEPS, drain, 0)


def draft(nt, nd, picked, draft_weight):
    rows, cols = picked.shape
    depth = draft_weight.shape[0]
    minors = nd // nt
    dma = pltpu.SemaphoreType.DMA
    return pl.pallas_call(
        functools.partial(draft_kernel, nt, nd),
        out_shape=jax.ShapeDtypeStruct((STEPS, rows, cols), BF16),
        in_specs=[pl.BlockSpec(memory_space=pltpu.VMEM), pl.BlockSpec(memory_space=pl.ANY)],
        out_specs=pl.BlockSpec(memory_space=pltpu.VMEM),
        scratch_shapes=[
            pltpu.VMEM((depth, cols), BF16),
            pltpu.VMEM((STEPS + 1, rows, cols), BF16),
            pltpu.VMEM((STEPS, nt - 1, rows, cols), BF16),
            pltpu.VMEM((STEPS, nt * rows, depth), BF16),
            pltpu.VMEM((nt * rows, cols), F32),
            pltpu.VMEM((STEPS, nt * rows, cols), BF16),
            pltpu.VMEM((STEPS, nt - 1, rows, cols), BF16),
            dma,
            dma((STEPS, nt - 1)),
            dma((STEPS, nt - 1)),
            dma((STEPS, nt, minors)),
            dma((STEPS, nt, minors)),
            dma((STEPS, nt - 1)),
            dma((STEPS, nt - 1)),
        ],
        compiler_params=pltpu.CompilerParams(
            collective_id=0, has_side_effects=True, vmem_limit_bytes=40 * 1024 * 1024
        ),
        cost_estimate=pl.CostEstimate(
            flops=2 * STEPS * nt * rows * depth * cols,
            bytes_accessed=2 * depth * cols,
            transcendentals=STEPS * rows * cols,
        ),
    )(picked, draft_weight)


def per_device(
    queries,
    new_keys,
    new_values,
    key_cache,
    value_cache,
    cache_lengths,
    accepted,
    residual,
    out_weight,
    draft_weight,
):
    windows_here, tokens_here, query_width = queries.shape
    cache_size = key_cache.shape[1]
    kv_here = new_keys.shape[2] // HD
    group_size = query_width // HD // kv_here
    query_split = queries.reshape(windows_here, tokens_here, kv_here, group_size, HD)
    keys_cached = key_cache.reshape(windows_here, cache_size, kv_here, HD)
    keys_fresh = new_keys.reshape(windows_here, tokens_here, kv_here, HD)
    score_cache = jnp.einsum(
        "wtkgd,wpkd->wkgtp", query_split, keys_cached, preferred_element_type=jnp.float32
    ) * HD ** (-0.5)
    score_fresh = jnp.einsum(
        "wtkgd,wpkd->wkgtp", query_split, keys_fresh, preferred_element_type=jnp.float32
    ) * HD ** (-0.5)
    live_cache = (jnp.arange(cache_size)[None, :] < cache_lengths[:, None])[:, None, None, None, :]
    live_fresh = jnp.arange(tokens_here)[None, :] <= jnp.arange(tokens_here)[:, None]
    scores = jnp.concatenate(
        [
            jnp.where(live_cache, score_cache, -jnp.inf),
            jnp.where(live_fresh, score_fresh, -jnp.inf),
        ],
        axis=-1,
    )
    largest = jnp.max(scores, axis=-1, keepdims=True)
    powered = jnp.exp(scores - largest)
    weights = (powered / jnp.sum(powered, axis=-1, keepdims=True)).astype(jnp.bfloat16)
    values_cached = value_cache.reshape(windows_here, cache_size, kv_here, HD)
    values_fresh = new_values.reshape(windows_here, tokens_here, kv_here, HD)
    mixed_rows = jnp.einsum(
        "wkgtp,wpkd->wtkgd",
        weights[..., :cache_size],
        values_cached,
        preferred_element_type=jnp.float32,
    )
    mixed_rows = mixed_rows + jnp.einsum(
        "wkgtp,wpkd->wtkgd",
        weights[..., cache_size:],
        values_fresh,
        preferred_element_type=jnp.float32,
    )
    attended = mixed_rows.astype(jnp.bfloat16).reshape(windows_here * tokens_here, query_width)
    partial_out = jnp.dot(
        lax.all_gather(attended, "dp", axis=0, tiled=True),
        out_weight,
        preferred_element_type=jnp.float32,
    )
    summed = lax.psum_scatter(partial_out, "tensor", scatter_dimension=0, tiled=True)
    block_windows, block_tokens, block_cols = residual.shape
    flat_residual = residual.reshape(block_windows * block_tokens, block_cols).astype(jnp.float32)
    verified = (
        (flat_residual + summed)
        .astype(jnp.bfloat16)
        .reshape(block_windows, block_tokens, block_cols)
    )
    chosen = jnp.arange(block_tokens)[None, :] == (accepted - 1)[:, None]
    picked = jnp.sum(
        jnp.where(chosen[:, :, None], verified, jnp.zeros((), jnp.bfloat16)),
        axis=1,
        dtype=jnp.bfloat16,
    )
    drafted = draft(lax.axis_size("tensor"), lax.axis_size("dp"), picked, draft_weight)
    return (verified, drafted)


def solution(mesh):
    placed = (
        P("dp", None, "tensor"),
        P("dp", None, "tensor"),
        P("dp", None, "tensor"),
        P("dp", None, "tensor"),
        P("dp", None, "tensor"),
        P("dp"),
        P("tensor"),
        P("tensor", None, "dp"),
        P("tensor", "dp"),
        P("tensor", "dp"),
    )
    return jax.shard_map(
        per_device,
        mesh=mesh,
        in_specs=placed,
        out_specs=(P("tensor", None, "dp"), P(None, "tensor", "dp")),
        check_vma=False,
    )
```

```python
import functools

import jax
import jax.numpy as jnp
from jax import lax
from jax.experimental import pallas as pl
from jax.experimental.pallas import tpu as pltpu
from jax.sharding import PartitionSpec as P

HD = 128
STEPS = 5


MESH = pl.DeviceIdType.MESH
BF16 = jnp.bfloat16
F32 = jnp.float32


def decode_kernel(
    nt,
    nd,
    attended_ref,
    accepted_ref,
    residual_ref,
    out_weight_hbm,
    draft_weight_hbm,
    verified_ref,
    drafted_ref,
    out_weight,
    draft_weight,
    accepted_near,
    first,
    pieces,
    spread,
    feats,
    partial,
    outgoing,
    landed,
    rows_all,
    rows_own,
    rows_out,
    rows_in,
    weight_sem,
    accepted_send,
    accepted_recv,
    first_send,
    first_pass,
    first_recv,
    spread_send,
    spread_recv,
    feat_send,
    feat_recv,
    part_send,
    part_recv,
    all_send,
    all_pass,
    all_recv,
    rows_send,
    rows_recv,
):
    rows, cols = pieces.shape[1:]
    minors = nd // nt
    windows = rows // minors
    held, depth = attended_ref.shape
    tokens = held // windows
    half = depth // 2
    me_t = lax.axis_index("tensor")
    me_d = lax.axis_index("dp")
    group = me_d // minors
    minor = me_d % minors
    order = sorted(range(nt), key=lambda i: min(i, nt - i))

    load_out = pltpu.make_async_copy(out_weight_hbm, out_weight, weight_sem.at[0])
    load_draft = pltpu.make_async_copy(draft_weight_hbm, draft_weight, weight_sem.at[1])
    load_out.start()
    load_draft.start()
    barrier = pltpu.get_barrier_semaphore()
    for k in range(nt):
        for j in range(minors):
            if k or j:
                peer = (group * minors + (minor + j) % minors, (me_t + k) % nt)
                pl.semaphore_signal(barrier, inc=1, device_id=peer, device_id_type=MESH)
    for i in range(1, nt):
        peer = ((group + i) % nt * minors + minor, me_t)
        pl.semaphore_signal(barrier, inc=1, device_id=peer, device_id_type=MESH)
    pl.semaphore_wait(barrier, nt * minors - 1 + nt - 1)

    def accepted_copy(k):
        return pltpu.make_async_remote_copy(
            src_ref=accepted_ref,
            dst_ref=accepted_near,
            send_sem=accepted_send.at[k - 1],
            recv_sem=accepted_recv,
            device_id=(me_d, (me_t + k) % nt),
            device_id_type=MESH,
        )

    accepted_local = pltpu.make_async_copy(accepted_ref, accepted_near, accepted_recv)

    @pl.when(me_t == group)
    def _():
        for k in range(1, nt):
            accepted_copy(k).start()
        accepted_local.start()

    rows_all[pl.ds(pl.multiple_of(me_d * held, held), held), :] = attended_ref[...]

    def pick(counts, count, table):
        place = lax.broadcasted_iota(jnp.int32, (count, table.shape[0]), 1).astype(F32)
        window = lax.broadcasted_iota(jnp.int32, (count, table.shape[0]), 0).astype(F32)
        chosen = place == window * tokens + (counts - 1.0)
        return jnp.dot(
            jnp.where(chosen, 1.0, 0.0).astype(BF16), table, preferred_element_type=F32
        )

    accepted_local.wait()
    near = accepted_near[pl.ds(pl.multiple_of(minor * windows, windows), windows), 0:1]
    picked = pick(near, windows, attended_ref[...])
    first[pl.ds(pl.multiple_of(me_d * 2 * windows, 2 * windows), 2 * windows), :] = (
        jnp.concatenate([picked[:, :half], picked[:, half:]], axis=0).astype(BF16)
    )

    def block_of(ref, i, j, block):
        source = (group + nt - i) % nt * minors + (minor + minors - j) % minors
        return ref.at[pl.ds(pl.multiple_of(source * block, block), block)], source

    def group_copy(ref, block, send, recv, i):
        slot, source = block_of(ref, 0, 0, block)
        return pltpu.make_async_remote_copy(
            src_ref=slot,
            dst_ref=slot,
            send_sem=send.at[i - 1],
            recv_sem=recv.at[source],
            device_id=((group + i) % nt * minors + minor, me_t),
            device_id_type=MESH,
        )

    def member_copy(ref, block, send, recv, i, j):
        slot, source = block_of(ref, i, 0, block)
        return pltpu.make_async_remote_copy(
            src_ref=slot,
            dst_ref=slot,
            send_sem=send.at[i, j - 1],
            recv_sem=recv.at[source],
            device_id=(group * minors + (minor + j) % minors, me_t),
            device_id_type=MESH,
        )

    def arrived(ref, block, recv, i, j):
        slot, source = block_of(ref, i, j, block)
        pltpu.make_async_copy(slot, slot, recv.at[source]).wait()

    first_group = functools.partial(group_copy, first, 2 * windows, first_send, first_recv)
    first_member = functools.partial(member_copy, first, 2 * windows, first_pass, first_recv)
    first_arrived = functools.partial(arrived, first, 2 * windows, first_recv)
    all_group = functools.partial(group_copy, rows_all, held, all_send, all_recv)
    all_member = functools.partial(member_copy, rows_all, held, all_pass, all_recv)
    all_arrived = functools.partial(arrived, rows_all, held, all_recv)

    def spread_copy(s, i):
        return pltpu.make_async_remote_copy(
            src_ref=pieces.at[s],
            dst_ref=spread.at[s, i - 1],
            send_sem=spread_send.at[s, i - 1],
            recv_sem=spread_recv.at[s, i - 1],
            device_id=((group + i) % nt * minors + minor, me_t),
            device_id_type=MESH,
        )

    def feat_slot(s):
        return feats.at[
            s,
            pl.ds(pl.multiple_of(me_t * rows, rows), rows),
            pl.ds(pl.multiple_of(minor * cols, cols), cols),
        ]

    def feat_copy(s, i, j):
        return pltpu.make_async_remote_copy(
            src_ref=pieces.at[s] if i == 0 else spread.at[s, i - 1],
            dst_ref=feat_slot(s),
            send_sem=feat_send.at[s, i, j],
            recv_sem=feat_recv.at[s, me_t, minor],
            device_id=(group * minors + (minor + j) % minors, (group + nt - i) % nt),
            device_id_type=MESH,
        )

    def feat_local(s, i):
        return pltpu.make_async_copy(
            pieces.at[s] if i == 0 else spread.at[s, i - 1],
            feat_slot(s),
            feat_recv.at[s, me_t, minor],
        )

    def part_copy(s, k):
        return pltpu.make_async_remote_copy(
            src_ref=outgoing.at[s, pl.ds(pl.multiple_of((me_t + k) % nt * rows, rows), rows)],
            dst_ref=landed.at[s, k - 1],
            send_sem=part_send.at[s, k - 1],
            recv_sem=part_recv.at[s, k - 1],
            device_id=(me_d, (me_t + k) % nt),
            device_id_type=MESH,
        )

    def summed(s):
        for k in range(1, nt):
            part_copy(s, k).start()
        total = partial[pl.ds(pl.multiple_of(me_t * rows, rows), rows), :]
        for k in range(1, nt):
            part_copy(s, k).wait_recv()
            total = total + landed[s, k - 1].astype(F32)
        return total

    for i in order[1:]:
        first_group(i).start()
    for i in order:
        if i:
            first_arrived(i, 0)
        for j in range(1, minors):
            first_member(i, j).start()
    residual_picked = pick(accepted_ref[:, 0:1], rows, residual_ref[...])
    load_out.wait()
    for i in order:
        for j in range(1, minors):
            first_arrived(i, j)
    for c in range(0, cols, 256):
        low = jnp.dot(first[...], out_weight[:half, c : c + 256], preferred_element_type=F32)
        high = jnp.dot(first[...], out_weight[half:, c : c + 256], preferred_element_type=F32)
        product = (
            low.reshape(nd, 2, windows, 256)[:, 0] + high.reshape(nd, 2, windows, 256)[:, 1]
        ).reshape(nd * windows, 256)
        partial[:, c : c + 256] = product
        outgoing[STEPS, :, c : c + 256] = product.astype(BF16)
    pieces[0] = (residual_picked + summed(STEPS)).astype(BF16)
    load_draft.wait()

    def rows_copy(i):
        return pltpu.make_async_remote_copy(
            src_ref=rows_out.at[i],
            dst_ref=rows_in.at[me_t],
            send_sem=rows_send.at[i],
            recv_sem=rows_recv.at[me_t],
            device_id=(me_d, (group + nt - i) % nt),
            device_id_type=MESH,
        )

    def project(i):
        for j in range(1, minors):
            all_arrived(i, j)
        target = (group + nt - i) % nt
        span = minors * held
        block = rows_all.at[pl.ds(pl.multiple_of(target * span, span), span)]
        for c in range(0, cols, 256):
            product = jnp.dot(block[...], out_weight[:, c : c + 256], preferred_element_type=F32)
            rows_out[i, :, c : c + 256] = product.astype(BF16)

            @pl.when(target == me_t)
            def _():
                rows_own[:, c : c + 256] = product

        @pl.when(target != me_t)
        def _():
            rows_copy(i).start()

    def forward(i):
        all_arrived(i, 0)
        for j in range(1, minors):
            all_member(i, j).start()

    def collect():
        for k in range(1, nt):
            source = (me_t + k) % nt
            slot = rows_in.at[source]
            pltpu.make_async_copy(slot, slot, rows_recv.at[source]).wait()
        for c in range(0, cols, 256):
            total = rows_own[:, c : c + 256] + residual_ref[:, c : c + 256].astype(F32)
            for k in range(1, nt):
                total = total + rows_in[(me_t + k) % nt, :, c : c + 256].astype(F32)
            verified_ref[:, c : c + 256] = total.astype(BF16)

    close = nt // 2 + 1

    def background(s):
        @pl.when(s == 0)
        def _():
            for i in order[1:]:
                all_group(i).start()
            for j in range(1, minors):
                all_member(0, j).start()

        @pl.when(s == 1)
        def _():
            project(order[0])
            for i in order[1:close]:
                forward(i)

        @pl.when(s == 2)
        def _():
            project(order[1])
            for i in order[close:]:
                forward(i)

        @pl.when(s == 3)
        def _():
            for i in order[2:]:
                project(i)

        @pl.when(s == STEPS - 1)
        def _():
            collect()

    def step(s, carry):
        for i in order[1:]:
            spread_copy(s, i).start()
        for i in order:
            if i:
                spread_copy(s, i).wait_recv()
            target = (group + nt - i) % nt
            for j in range(1, minors):
                feat_copy(s, i, j).start()

            @pl.when(target != me_t)
            def _():
                feat_copy(s, i, 0).start()

            @pl.when(target == me_t)
            def _():
                feat_local(s, i).start()

            if i == 0:
                background(s)

        for t in range(nt):
            for m in range(minors):
                pltpu.make_async_copy(
                    pieces.at[s],
                    feats.at[s, pl.ds(t * rows, rows), pl.ds(m * cols, cols)],
                    feat_recv.at[s, t, m],
                ).wait()
        for c in range(0, cols, 256):
            product = jnp.dot(
                feats[s], draft_weight[:, c : c + 256], preferred_element_type=F32
            )
            partial[:, c : c + 256] = product
            outgoing[s, :, c : c + 256] = product.astype(BF16)
        drafted = jnp.tanh(2.0 * summed(s)).astype(BF16)
        drafted_ref[s] = drafted
        pieces[s + 1] = drafted
        return carry

    lax.fori_loop(0, STEPS, step, 0)

    def drain(s, carry):
        for i in range(nt):
            if i:
                spread_copy(s, i).wait_send()
                part_copy(s, i).wait_send()
            for j in range(1, minors):
                feat_copy(s, i, j).wait_send()

            @pl.when((group + nt - i) % nt != me_t)
            def _():
                feat_copy(s, i, 0).wait_send()

        return carry

    lax.fori_loop(0, STEPS, drain, 0)
    for i in range(nt):
        if i:
            part_copy(STEPS, i).wait_send()
            first_group(i).wait_send()
            all_group(i).wait_send()
        for j in range(1, minors):
            first_member(i, j).wait_send()
            all_member(i, j).wait_send()

        @pl.when((group + nt - i) % nt != me_t)
        def _():
            rows_copy(i).wait_send()

    @pl.when(me_t == group)
    def _():
        for k in range(1, nt):
            accepted_copy(k).wait_send()


def decode(nt, nd, attended, accepted, residual, out_weight, draft_weight):
    held, depth = attended.shape
    span, cols = residual.shape
    rows = accepted.shape[0]
    minors = nd // nt
    windows = rows // minors
    dma = pltpu.SemaphoreType.DMA
    vmem = pl.BlockSpec(memory_space=pltpu.VMEM)
    hbm = pl.BlockSpec(memory_space=pl.ANY)
    return pl.pallas_call(
        functools.partial(decode_kernel, nt, nd),
        out_shape=(
            jax.ShapeDtypeStruct((span, cols), BF16),
            jax.ShapeDtypeStruct((STEPS, rows, cols), BF16),
        ),
        in_specs=[vmem, vmem, vmem, hbm, hbm],
        out_specs=(vmem, vmem),
        scratch_shapes=[
            pltpu.VMEM((depth, cols), BF16),
            pltpu.VMEM((depth, cols), BF16),
            pltpu.VMEM(accepted.shape, F32),
            pltpu.VMEM((nd * 2 * windows, depth // 2), BF16),
            pltpu.VMEM((STEPS + 1, rows, cols), BF16),
            pltpu.VMEM((STEPS, nt - 1, rows, cols), BF16),
            pltpu.VMEM((STEPS, nt * rows, depth), BF16),
            pltpu.VMEM((nt * rows, cols), F32),
            pltpu.VMEM((STEPS + 1, nt * rows, cols), BF16),
            pltpu.VMEM((STEPS + 1, nt - 1, rows, cols), BF16),
            pltpu.VMEM((nd * held, depth), BF16),
            pltpu.VMEM((span, cols), F32),
            pltpu.VMEM((nt, span, cols), BF16),
            pltpu.VMEM((nt, span, cols), BF16),
            dma((2,)),
            dma((nt - 1,)),
            dma,
            dma((nt - 1,)),
            dma((nt, minors - 1)),
            dma((nd,)),
            dma((STEPS, nt - 1)),
            dma((STEPS, nt - 1)),
            dma((STEPS, nt, minors)),
            dma((STEPS, nt, minors)),
            dma((STEPS + 1, nt - 1)),
            dma((STEPS + 1, nt - 1)),
            dma((nt - 1,)),
            dma((nt, minors - 1)),
            dma((nd,)),
            dma((nt,)),
            dma((nt,)),
        ],
        compiler_params=pltpu.CompilerParams(
            collective_id=0, has_side_effects=True, vmem_limit_bytes=48 * 1024 * 1024
        ),
        cost_estimate=pl.CostEstimate(
            flops=2 * (STEPS * nt * rows + nd * held) * depth * cols,
            bytes_accessed=4 * depth * cols,
            transcendentals=STEPS * rows * cols,
        ),
    )(attended, accepted, residual, out_weight, draft_weight)


def per_device(
    queries,
    new_keys,
    new_values,
    key_cache,
    value_cache,
    cache_lengths,
    accepted,
    residual,
    out_weight,
    draft_weight,
):
    windows_here, tokens_here, query_width = queries.shape
    cache_size = key_cache.shape[1]
    kv_here = new_keys.shape[2] // HD
    group_size = query_width // HD // kv_here
    query_split = queries.reshape(windows_here, tokens_here, kv_here, group_size, HD)
    keys_cached = key_cache.reshape(windows_here, cache_size, kv_here, HD)
    keys_fresh = new_keys.reshape(windows_here, tokens_here, kv_here, HD)
    score_cache = jnp.einsum(
        "wtkgd,wpkd->wkgtp", query_split, keys_cached, preferred_element_type=jnp.float32
    ) * HD ** (-0.5)
    score_fresh = jnp.einsum(
        "wtkgd,wpkd->wkgtp", query_split, keys_fresh, preferred_element_type=jnp.float32
    ) * HD ** (-0.5)
    live_cache = (jnp.arange(cache_size)[None, :] < cache_lengths[:, None])[:, None, None, None, :]
    live_fresh = jnp.arange(tokens_here)[None, :] <= jnp.arange(tokens_here)[:, None]
    scores = jnp.concatenate(
        [
            jnp.where(live_cache, score_cache, -jnp.inf),
            jnp.where(live_fresh, score_fresh, -jnp.inf),
        ],
        axis=-1,
    )
    largest = jnp.max(scores, axis=-1, keepdims=True)
    powered = jnp.exp(scores - largest)
    weights = (powered / jnp.sum(powered, axis=-1, keepdims=True)).astype(jnp.bfloat16)
    values_cached = value_cache.reshape(windows_here, cache_size, kv_here, HD)
    values_fresh = new_values.reshape(windows_here, tokens_here, kv_here, HD)
    mixed_rows = jnp.einsum(
        "wkgtp,wpkd->wtkgd",
        weights[..., :cache_size],
        values_cached,
        preferred_element_type=jnp.float32,
    )
    mixed_rows = mixed_rows + jnp.einsum(
        "wkgtp,wpkd->wtkgd",
        weights[..., cache_size:],
        values_fresh,
        preferred_element_type=jnp.float32,
    )
    attended = mixed_rows.astype(jnp.bfloat16).reshape(windows_here * tokens_here, query_width)
    block_windows, block_tokens, block_cols = residual.shape
    verified, drafted = decode(
        lax.axis_size("tensor"),
        lax.axis_size("dp"),
        attended,
        jnp.broadcast_to(accepted.astype(F32)[:, None], (block_windows, HD)),
        residual.reshape(block_windows * block_tokens, block_cols),
        out_weight,
        draft_weight,
    )
    return (verified.reshape(residual.shape), drafted)


def solution(mesh):
    placed = (
        P("dp", None, "tensor"),
        P("dp", None, "tensor"),
        P("dp", None, "tensor"),
        P("dp", None, "tensor"),
        P("dp", None, "tensor"),
        P("dp"),
        P("tensor"),
        P("tensor", None, "dp"),
        P("tensor", "dp"),
        P("tensor", "dp"),
    )
    return jax.shard_map(
        per_device,
        mesh=mesh,
        in_specs=placed,
        out_specs=(P("tensor", None, "dp"), P(None, "tensor", "dp")),
        check_vma=False,
    )
```

```python
import functools

import jax
import jax.numpy as jnp
from jax import lax
from jax.experimental import pallas as pl
from jax.experimental.pallas import tpu as pltpu
from jax.sharding import PartitionSpec as P

HD = 128
STEPS = 5
CUTS = 2


MESH = pl.DeviceIdType.MESH
BF16 = jnp.bfloat16
F32 = jnp.float32


def decode_kernel(
    nt,
    nd,
    attended_ref,
    accepted_ref,
    residual_ref,
    out_weight_hbm,
    draft_weight_hbm,
    verified_ref,
    drafted_ref,
    out_weight,
    draft_weight,
    accepted_near,
    first,
    pieces,
    spread,
    feats,
    partial,
    outgoing,
    landed,
    rows_all,
    rows_own,
    rows_out,
    rows_in,
    weight_sem,
    accepted_send,
    accepted_recv,
    first_send,
    first_pass,
    first_recv,
    spread_send,
    spread_recv,
    feat_send,
    feat_recv,
    part_send,
    part_recv,
    all_send,
    all_pass,
    all_recv,
    rows_send,
    rows_recv,
):
    rows, part = pieces.shape[2:]
    cols = part * CUTS
    chunk = min(part, 256)
    minors = nd // nt
    windows = rows // minors
    held, depth = attended_ref.shape
    tokens = held // windows
    half = depth // 2
    me_t = lax.axis_index("tensor")
    me_d = lax.axis_index("dp")
    group = me_d // minors
    minor = me_d % minors
    order = sorted(range(nt), key=lambda i: min(i, nt - i))
    spans = max(1, STEPS - 2)
    turns = [
        [i for q, i in enumerate(order[1:]) if q * spans // (nt - 1) == turn]
        for turn in range(spans)
    ]

    load_out = pltpu.make_async_copy(out_weight_hbm, out_weight, weight_sem.at[0])
    load_draft = pltpu.make_async_copy(draft_weight_hbm, draft_weight, weight_sem.at[1])
    load_out.start()
    load_draft.start()
    barrier = pltpu.get_barrier_semaphore()
    for k in range(nt):
        for j in range(minors):
            if k or j:
                peer = (group * minors + (minor + j) % minors, (me_t + k) % nt)
                pl.semaphore_signal(barrier, inc=1, device_id=peer, device_id_type=MESH)
    for i in range(1, nt):
        peer = ((group + i) % nt * minors + minor, me_t)
        pl.semaphore_signal(barrier, inc=1, device_id=peer, device_id_type=MESH)
    pl.semaphore_wait(barrier, nt * minors - 1 + nt - 1)

    def accepted_copy(k):
        return pltpu.make_async_remote_copy(
            src_ref=accepted_ref,
            dst_ref=accepted_near,
            send_sem=accepted_send.at[k - 1],
            recv_sem=accepted_recv,
            device_id=(me_d, (me_t + k) % nt),
            device_id_type=MESH,
        )

    accepted_local = pltpu.make_async_copy(accepted_ref, accepted_near, accepted_recv)

    @pl.when(me_t == group)
    def _():
        for k in range(1, nt):
            accepted_copy(k).start()
        accepted_local.start()

    rows_all[pl.ds(pl.multiple_of(me_d * held, held), held), :] = attended_ref[...]

    def pick(counts, count, table):
        place = lax.broadcasted_iota(jnp.int32, (count, table.shape[0]), 1).astype(F32)
        window = lax.broadcasted_iota(jnp.int32, (count, table.shape[0]), 0).astype(F32)
        chosen = place == window * tokens + (counts - 1.0)
        return jnp.dot(
            jnp.where(chosen, 1.0, 0.0).astype(BF16), table, preferred_element_type=F32
        )

    accepted_local.wait()
    near = accepted_near[pl.ds(pl.multiple_of(minor * windows, windows), windows), 0:1]
    picked = pick(near, windows, attended_ref[...])
    first[pl.ds(pl.multiple_of(me_d * 2 * windows, 2 * windows), 2 * windows), :] = (
        jnp.concatenate([picked[:, :half], picked[:, half:]], axis=0).astype(BF16)
    )

    def block_of(ref, i, j, block):
        source = (group + nt - i) % nt * minors + (minor + minors - j) % minors
        return ref.at[pl.ds(pl.multiple_of(source * block, block), block)], source

    def group_copy(ref, block, send, recv, i):
        slot, source = block_of(ref, 0, 0, block)
        return pltpu.make_async_remote_copy(
            src_ref=slot,
            dst_ref=slot,
            send_sem=send.at[i - 1],
            recv_sem=recv.at[source],
            device_id=((group + i) % nt * minors + minor, me_t),
            device_id_type=MESH,
        )

    def member_copy(ref, block, send, recv, i, j):
        slot, source = block_of(ref, i, 0, block)
        return pltpu.make_async_remote_copy(
            src_ref=slot,
            dst_ref=slot,
            send_sem=send.at[i, j - 1],
            recv_sem=recv.at[source],
            device_id=(group * minors + (minor + j) % minors, me_t),
            device_id_type=MESH,
        )

    def arrived(ref, block, recv, i, j):
        slot, source = block_of(ref, i, j, block)
        pltpu.make_async_copy(slot, slot, recv.at[source]).wait()

    first_group = functools.partial(group_copy, first, 2 * windows, first_send, first_recv)
    first_member = functools.partial(member_copy, first, 2 * windows, first_pass, first_recv)
    first_arrived = functools.partial(arrived, first, 2 * windows, first_recv)
    all_group = functools.partial(group_copy, rows_all, held, all_send, all_recv)
    all_member = functools.partial(member_copy, rows_all, held, all_pass, all_recv)
    all_arrived = functools.partial(arrived, rows_all, held, all_recv)

    def spread_copy(s, h, i):
        return pltpu.make_async_remote_copy(
            src_ref=pieces.at[s, h],
            dst_ref=spread.at[s, h, i - 1],
            send_sem=spread_send.at[s, h, i - 1],
            recv_sem=spread_recv.at[s, h, i - 1],
            device_id=((group + i) % nt * minors + minor, me_t),
            device_id_type=MESH,
        )

    def feat_slot(s, h):
        return feats.at[
            s,
            h,
            pl.ds(pl.multiple_of(me_t * rows, rows), rows),
            pl.ds(pl.multiple_of(minor * part, part), part),
        ]

    def feat_copy(s, h, i, j):
        return pltpu.make_async_remote_copy(
            src_ref=pieces.at[s, h] if i == 0 else spread.at[s, h, i - 1],
            dst_ref=feat_slot(s, h),
            send_sem=feat_send.at[s, h, i, j],
            recv_sem=feat_recv.at[s, h, me_t, minor],
            device_id=(group * minors + (minor + j) % minors, (group + nt - i) % nt),
            device_id_type=MESH,
        )

    def feat_local(s, h, i):
        return pltpu.make_async_copy(
            pieces.at[s, h] if i == 0 else spread.at[s, h, i - 1],
            feat_slot(s, h),
            feat_recv.at[s, h, me_t, minor],
        )

    def deliver(s, h, i):
        target = (group + nt - i) % nt
        for j in range(1, minors):
            feat_copy(s, h, i, j).start()

        @pl.when(target != me_t)
        def _():
            feat_copy(s, h, i, 0).start()

        @pl.when(target == me_t)
        def _():
            feat_local(s, h, i).start()

    def launch(s, h):
        for i in order[1:]:
            spread_copy(s, h, i).start()
        deliver(s, h, 0)

    def part_copy(s, n, k):
        return pltpu.make_async_remote_copy(
            src_ref=outgoing.at[s, n, pl.ds(pl.multiple_of((me_t + k) % nt * rows, rows), rows)],
            dst_ref=landed.at[s, n, k - 1],
            send_sem=part_send.at[s, n, k - 1],
            recv_sem=part_recv.at[s, n, k - 1],
            device_id=(me_d, (me_t + k) % nt),
            device_id_type=MESH,
        )

    def share(s, n):
        for k in range(1, nt):
            part_copy(s, n, k).start()

    def summed(s, n):
        total = partial[n, pl.ds(pl.multiple_of(me_t * rows, rows), rows), :]
        for k in range(1, nt):
            part_copy(s, n, k).wait_recv()
            total = total + landed[s, n, k - 1].astype(F32)
        return total

    for i in order[1:]:
        first_group(i).start()
    for j in range(1, minors):
        all_member(0, j).start()
    for i in order:
        if i:
            first_arrived(i, 0)
        for j in range(1, minors):
            first_member(i, j).start()
    for i in turns[0]:
        all_group(i).start()
    residual_picked = pick(accepted_ref[:, 0:1], rows, residual_ref[...])
    load_out.wait()
    for i in order:
        for j in range(1, minors):
            first_arrived(i, j)
    for n in range(CUTS):
        for c in range(0, part, chunk):
            lanes = pl.ds(n * part + c, chunk)
            low = jnp.dot(first[...], out_weight[:half, lanes], preferred_element_type=F32)
            high = jnp.dot(first[...], out_weight[half:, lanes], preferred_element_type=F32)
            product = (
                low.reshape(nd, 2, windows, chunk)[:, 0]
                + high.reshape(nd, 2, windows, chunk)[:, 1]
            ).reshape(nd * windows, chunk)
            partial[n, :, c : c + chunk] = product
            outgoing[STEPS, n, :, c : c + chunk] = product.astype(BF16)
        share(STEPS, n)
    for n in range(CUTS):
        pieces[0, n] = (
            residual_picked[:, n * part : (n + 1) * part] + summed(STEPS, n)
        ).astype(BF16)
        launch(0, n)
    load_draft.wait()

    def rows_copy(i):
        return pltpu.make_async_remote_copy(
            src_ref=rows_out.at[i],
            dst_ref=rows_in.at[me_t],
            send_sem=rows_send.at[i],
            recv_sem=rows_recv.at[me_t],
            device_id=(me_d, (group + nt - i) % nt),
            device_id_type=MESH,
        )

    def project(i):
        for j in range(1, minors):
            all_arrived(i, j)
        target = (group + nt - i) % nt
        span = minors * held
        block = rows_all.at[pl.ds(pl.multiple_of(target * span, span), span)]
        for c in range(0, cols, 256):
            product = jnp.dot(block[...], out_weight[:, c : c + 256], preferred_element_type=F32)
            rows_out[i, :, c : c + 256] = product.astype(BF16)

            @pl.when(target == me_t)
            def _():
                rows_own[:, c : c + 256] = product

        @pl.when(target != me_t)
        def _():
            rows_copy(i).start()

    def forward(i):
        all_arrived(i, 0)
        for j in range(1, minors):
            all_member(i, j).start()

    def collect():
        for k in range(1, nt):
            source = (me_t + k) % nt
            slot = rows_in.at[source]
            pltpu.make_async_copy(slot, slot, rows_recv.at[source]).wait()
        for c in range(0, cols, 256):
            total = rows_own[:, c : c + 256] + residual_ref[:, c : c + 256].astype(F32)
            for k in range(1, nt):
                total = total + rows_in[(me_t + k) % nt, :, c : c + 256].astype(F32)
            verified_ref[:, c : c + 256] = total.astype(BF16)

    def early(s):
        for turn in range(spans + 1):

            @pl.when(s == turn)
            def _(turn=turn):
                for i in turns[turn] if turn < spans else []:
                    forward(i)
                for i in turns[turn - 1] if turn else order[:1]:
                    project(i)

        @pl.when(s == spans + 1)
        def _():
            collect()

    def late(s):
        for turn in range(1, spans):

            @pl.when(s == turn - 1)
            def _(turn=turn):
                for i in turns[turn]:
                    all_group(i).start()

    def step(s, carry):
        early(s)
        for h in range(CUTS):
            for i in order[1:]:
                spread_copy(s, h, i).wait_recv()
                deliver(s, h, i)
        late(s)
        for h in range(CUTS):
            for t in range(nt):
                for m in range(minors):
                    pltpu.make_async_copy(
                        pieces.at[s, h],
                        feats.at[s, h, pl.ds(t * rows, rows), pl.ds(m * part, part)],
                        feat_recv.at[s, h, t, m],
                    ).wait()
            for n in range(CUTS):
                for c in range(0, part, chunk):
                    product = sum(
                        jnp.dot(
                            feats[s, h, :, m * part : (m + 1) * part],
                            draft_weight[
                                pl.ds(m * cols + h * part, part), pl.ds(n * part + c, chunk)
                            ],
                            preferred_element_type=F32,
                        )
                        for m in range(minors)
                    )
                    if h:
                        product = product + partial[n, :, c : c + chunk]
                    partial[n, :, c : c + chunk] = product
                    if h == CUTS - 1:
                        outgoing[s, n, :, c : c + chunk] = product.astype(BF16)
                if h == CUTS - 1:
                    share(s, n)
        for n in range(CUTS):
            drafted = jnp.tanh(2.0 * summed(s, n)).astype(BF16)
            drafted_ref[s, :, n * part : (n + 1) * part] = drafted
            pieces[s + 1, n] = drafted

            @pl.when(s < STEPS - 1)
            def _():
                launch(s + 1, n)

        return carry

    lax.fori_loop(0, STEPS, step, 0)

    def drain(s, carry):
        for h in range(CUTS):
            for i in range(nt):
                if i:
                    spread_copy(s, h, i).wait_send()
                    part_copy(s, h, i).wait_send()
                for j in range(1, minors):
                    feat_copy(s, h, i, j).wait_send()

                @pl.when((group + nt - i) % nt != me_t)
                def _():
                    feat_copy(s, h, i, 0).wait_send()

        return carry

    lax.fori_loop(0, STEPS, drain, 0)
    for i in range(nt):
        if i:
            for n in range(CUTS):
                part_copy(STEPS, n, i).wait_send()
            first_group(i).wait_send()
            all_group(i).wait_send()
        for j in range(1, minors):
            first_member(i, j).wait_send()
            all_member(i, j).wait_send()

        @pl.when((group + nt - i) % nt != me_t)
        def _():
            rows_copy(i).wait_send()

    @pl.when(me_t == group)
    def _():
        for k in range(1, nt):
            accepted_copy(k).wait_send()


def decode(nt, nd, attended, accepted, residual, out_weight, draft_weight):
    held, depth = attended.shape
    span, cols = residual.shape
    rows = accepted.shape[0]
    minors = nd // nt
    windows = rows // minors
    part = cols // CUTS
    dma = pltpu.SemaphoreType.DMA
    vmem = pl.BlockSpec(memory_space=pltpu.VMEM)
    hbm = pl.BlockSpec(memory_space=pltpu.HBM)
    return pl.pallas_call(
        functools.partial(decode_kernel, nt, nd),
        out_shape=(
            jax.ShapeDtypeStruct((span, cols), BF16),
            jax.ShapeDtypeStruct((STEPS, rows, cols), BF16),
        ),
        in_specs=[vmem, vmem, vmem, hbm, hbm],
        out_specs=(vmem, vmem),
        scratch_shapes=[
            pltpu.VMEM((depth, cols), BF16),
            pltpu.VMEM((depth, cols), BF16),
            pltpu.VMEM(accepted.shape, F32),
            pltpu.VMEM((nd * 2 * windows, depth // 2), BF16),
            pltpu.VMEM((STEPS + 1, CUTS, rows, part), BF16),
            pltpu.VMEM((STEPS, CUTS, nt - 1, rows, part), BF16),
            pltpu.VMEM((STEPS, CUTS, nt * rows, minors * part), BF16),
            pltpu.VMEM((CUTS, nt * rows, part), F32),
            pltpu.VMEM((STEPS + 1, CUTS, nt * rows, part), BF16),
            pltpu.VMEM((STEPS + 1, CUTS, nt - 1, rows, part), BF16),
            pltpu.VMEM((nd * held, depth), BF16),
            pltpu.VMEM((span, cols), F32),
            pltpu.VMEM((nt, span, cols), BF16),
            pltpu.VMEM((nt, span, cols), BF16),
            dma((2,)),
            dma((nt - 1,)),
            dma,
            dma((nt - 1,)),
            dma((nt, minors - 1)),
            dma((nd,)),
            dma((STEPS, CUTS, nt - 1)),
            dma((STEPS, CUTS, nt - 1)),
            dma((STEPS, CUTS, nt, minors)),
            dma((STEPS, CUTS, nt, minors)),
            dma((STEPS + 1, CUTS, nt - 1)),
            dma((STEPS + 1, CUTS, nt - 1)),
            dma((nt - 1,)),
            dma((nt, minors - 1)),
            dma((nd,)),
            dma((nt,)),
            dma((nt,)),
        ],
        compiler_params=pltpu.CompilerParams(
            collective_id=0, has_side_effects=True, vmem_limit_bytes=48 * 1024 * 1024
        ),
        cost_estimate=pl.CostEstimate(
            flops=2 * (STEPS * nt * rows + nd * held) * depth * cols,
            bytes_accessed=4 * depth * cols,
            transcendentals=STEPS * rows * cols,
        ),
    )(attended, accepted, residual, out_weight, draft_weight)


def per_device(
    queries,
    new_keys,
    new_values,
    key_cache,
    value_cache,
    cache_lengths,
    accepted,
    residual,
    out_weight,
    draft_weight,
):
    windows_here, tokens_here, query_width = queries.shape
    cache_size = key_cache.shape[1]
    kv_here = new_keys.shape[2] // HD
    group_size = query_width // HD // kv_here
    query_split = queries.reshape(windows_here, tokens_here, kv_here, group_size, HD)
    keys_cached = key_cache.reshape(windows_here, cache_size, kv_here, HD)
    keys_fresh = new_keys.reshape(windows_here, tokens_here, kv_here, HD)
    score_cache = jnp.einsum(
        "wtkgd,wpkd->wkgtp", query_split, keys_cached, preferred_element_type=jnp.float32
    ) * HD ** (-0.5)
    score_fresh = jnp.einsum(
        "wtkgd,wpkd->wkgtp", query_split, keys_fresh, preferred_element_type=jnp.float32
    ) * HD ** (-0.5)
    live_cache = (jnp.arange(cache_size)[None, :] < cache_lengths[:, None])[:, None, None, None, :]
    live_fresh = jnp.arange(tokens_here)[None, :] <= jnp.arange(tokens_here)[:, None]
    scores = jnp.concatenate(
        [
            jnp.where(live_cache, score_cache, -jnp.inf),
            jnp.where(live_fresh, score_fresh, -jnp.inf),
        ],
        axis=-1,
    )
    largest = jnp.max(scores, axis=-1, keepdims=True)
    powered = jnp.exp(scores - largest)
    weights = (powered / jnp.sum(powered, axis=-1, keepdims=True)).astype(jnp.bfloat16)
    values_cached = value_cache.reshape(windows_here, cache_size, kv_here, HD)
    values_fresh = new_values.reshape(windows_here, tokens_here, kv_here, HD)
    mixed_rows = jnp.einsum(
        "wkgtp,wpkd->wtkgd",
        weights[..., :cache_size],
        values_cached,
        preferred_element_type=jnp.float32,
    )
    mixed_rows = mixed_rows + jnp.einsum(
        "wkgtp,wpkd->wtkgd",
        weights[..., cache_size:],
        values_fresh,
        preferred_element_type=jnp.float32,
    )
    attended = mixed_rows.astype(jnp.bfloat16).reshape(windows_here * tokens_here, query_width)
    block_windows, block_tokens, block_cols = residual.shape
    verified, drafted = decode(
        lax.axis_size("tensor"),
        lax.axis_size("dp"),
        attended,
        jnp.broadcast_to(accepted.astype(F32)[:, None], (block_windows, HD)),
        residual.reshape(block_windows * block_tokens, block_cols),
        out_weight,
        draft_weight,
    )
    return (verified.reshape(residual.shape), drafted)


def solution(mesh):
    placed = (
        P("dp", None, "tensor"),
        P("dp", None, "tensor"),
        P("dp", None, "tensor"),
        P("dp", None, "tensor"),
        P("dp", None, "tensor"),
        P("dp"),
        P("tensor"),
        P("tensor", None, "dp"),
        P("tensor", "dp"),
        P("tensor", "dp"),
    )
    return jax.shard_map(
        per_device,
        mesh=mesh,
        in_specs=placed,
        out_specs=(P("tensor", None, "dp"), P(None, "tensor", "dp")),
        check_vma=False,
    )
```

```python
import functools

import jax
import jax.numpy as jnp
from jax import lax
from jax.experimental import pallas as pl
from jax.experimental.pallas import tpu as pltpu
from jax.sharding import PartitionSpec as P

HD = 128
STEPS = 5
CUTS = 2


MESH = pl.DeviceIdType.MESH
BF16 = jnp.bfloat16
F32 = jnp.float32


def decode_kernel(
    nt,
    nd,
    queries_ref,
    new_keys_ref,
    new_values_ref,
    lengths_ref,
    accepted_ref,
    residual_ref,
    key_cache_hbm,
    value_cache_hbm,
    out_weight_hbm,
    draft_weight_hbm,
    verified_ref,
    drafted_ref,
    out_weight,
    draft_weight,
    keys,
    values,
    query_pad,
    key_pad,
    value_pad,
    mixed,
    accepted_near,
    first,
    pieces,
    spread,
    feats,
    partial,
    outgoing,
    landed,
    rows_all,
    rows_own,
    rows_out,
    rows_in,
    weight_sem,
    accepted_send,
    accepted_recv,
    first_send,
    first_pass,
    first_recv,
    spread_send,
    spread_recv,
    feat_send,
    feat_recv,
    part_send,
    part_recv,
    all_send,
    all_pass,
    all_recv,
    rows_send,
    rows_recv,
):
    rows, part = pieces.shape[2:]
    cols = part * CUTS
    chunk = min(part, 256)
    minors = nd // nt
    windows, tokens, depth = queries_ref.shape
    held = windows * tokens
    cache = key_cache_hbm.shape[1]
    slots, kv_width = keys.shape[1:]
    token_pad = query_pad.shape[1]
    half = depth // 2
    me_t = lax.axis_index("tensor")
    me_d = lax.axis_index("dp")
    group = me_d // minors
    minor = me_d % minors
    order = sorted(range(nt), key=lambda i: min(i, nt - i))
    spans = max(1, STEPS - 2)
    turns = [
        [i for q, i in enumerate(order[1:]) if q * spans // (nt - 1) == turn]
        for turn in range(spans)
    ]

    load_out = pltpu.make_async_copy(out_weight_hbm, out_weight, weight_sem.at[0])
    load_draft = pltpu.make_async_copy(draft_weight_hbm, draft_weight, weight_sem.at[1])
    load_keys = pltpu.make_async_copy(
        key_cache_hbm, keys.at[:, pl.ds(0, cache)], weight_sem.at[2]
    )
    load_values = pltpu.make_async_copy(
        value_cache_hbm, values.at[:, pl.ds(0, cache)], weight_sem.at[3]
    )
    load_keys.start()
    load_values.start()
    load_out.start()
    load_draft.start()
    barrier = pltpu.get_barrier_semaphore()
    for k in range(nt):
        for j in range(minors):
            if k or j:
                peer = (group * minors + (minor + j) % minors, (me_t + k) % nt)
                pl.semaphore_signal(barrier, inc=1, device_id=peer, device_id_type=MESH)
    for i in range(1, nt):
        peer = ((group + i) % nt * minors + minor, me_t)
        pl.semaphore_signal(barrier, inc=1, device_id=peer, device_id_type=MESH)

    query_pad[...] = jnp.zeros_like(query_pad)
    key_pad[...] = jnp.zeros_like(key_pad)
    value_pad[...] = jnp.zeros_like(value_pad)
    query_pad[:, :tokens, :] = queries_ref[...].astype(F32)
    key_pad[:, :tokens, :] = new_keys_ref[...].astype(F32)
    value_pad[:, :tokens, :] = new_values_ref[...].astype(F32)
    keys[:, cache:, :] = key_pad[...].astype(BF16)
    values[:, cache:, :] = value_pad[...].astype(BF16)
    kv_heads = kv_width // HD
    share_heads = depth // kv_width
    query_rows = share_heads * token_pad
    spot = lax.broadcasted_iota(jnp.int32, (query_rows, slots), 1)
    token = lax.broadcasted_iota(jnp.int32, (query_rows, slots), 0) % token_pad
    fresh_live = (spot >= cache) & (spot - cache <= token)
    spot_float = spot.astype(F32)

    def attend(chosen_windows):
        units = [(w, k) for w in chosen_windows for k in range(kv_heads)]
        scores = []
        for w, k in units:
            heads = [
                query_pad[w, :, (k * share_heads + h) * HD : (k * share_heads + h + 1) * HD]
                for h in range(share_heads)
            ]
            scores.append(
                lax.dot_general(
                    jnp.concatenate(heads, axis=0).astype(BF16),
                    keys[w, :, k * HD : (k + 1) * HD],
                    (((1,), (1,)), ((), ())),
                    preferred_element_type=F32,
                )
                * HD ** (-0.5)
            )
        weights = []
        for (w, _), score in zip(units, scores):
            cached = (spot < cache) & (spot_float < lengths_ref[w : w + 1, 0:1])
            score = jnp.where(cached | fresh_live, score, -1e30)
            powered = jnp.exp(score - jnp.max(score, axis=-1, keepdims=True))
            weights.append(
                (powered * (1.0 / jnp.sum(powered, axis=-1, keepdims=True))).astype(BF16)
            )
        for (w, k), weight in zip(units, weights):
            result = jnp.dot(
                weight, values[w, :, k * HD : (k + 1) * HD], preferred_element_type=F32
            )
            for h in range(share_heads):
                head = k * share_heads + h
                mixed[w * token_pad : (w + 1) * token_pad, head * HD : (head + 1) * HD] = result[
                    h * token_pad : (h + 1) * token_pad
                ]

    load_keys.wait()
    load_values.wait()
    attend(range(windows // 2))
    pl.semaphore_wait(barrier, nt * minors - 1 + nt - 1)

    def accepted_copy(k):
        return pltpu.make_async_remote_copy(
            src_ref=accepted_ref,
            dst_ref=accepted_near,
            send_sem=accepted_send.at[k - 1],
            recv_sem=accepted_recv,
            device_id=(me_d, (me_t + k) % nt),
            device_id_type=MESH,
        )

    accepted_local = pltpu.make_async_copy(accepted_ref, accepted_near, accepted_recv)

    @pl.when(me_t == group)
    def _():
        for k in range(1, nt):
            accepted_copy(k).start()
        accepted_local.start()

    attend(range(windows // 2, windows))
    attended = mixed[...].astype(BF16)

    def pick(counts, count, table, tokens):
        place = lax.broadcasted_iota(jnp.int32, (count, table.shape[0]), 1).astype(F32)
        window = lax.broadcasted_iota(jnp.int32, (count, table.shape[0]), 0).astype(F32)
        chosen = place == window * tokens + (counts - 1.0)
        return jnp.dot(
            jnp.where(chosen, 1.0, 0.0).astype(BF16), table, preferred_element_type=F32
        )

    accepted_local.wait()
    near = accepted_near[pl.ds(pl.multiple_of(minor * windows, windows), windows), 0:1]
    picked = pick(near, windows, attended, token_pad)
    first[pl.ds(pl.multiple_of(me_d * 2 * windows, 2 * windows), 2 * windows), :] = (
        jnp.concatenate([picked[:, :half], picked[:, half:]], axis=0).astype(BF16)
    )

    def block_of(ref, i, j, block):
        source = (group + nt - i) % nt * minors + (minor + minors - j) % minors
        return ref.at[pl.ds(pl.multiple_of(source * block, block), block)], source

    def group_copy(ref, block, send, recv, i):
        slot, source = block_of(ref, 0, 0, block)
        return pltpu.make_async_remote_copy(
            src_ref=slot,
            dst_ref=slot,
            send_sem=send.at[i - 1],
            recv_sem=recv.at[source],
            device_id=((group + i) % nt * minors + minor, me_t),
            device_id_type=MESH,
        )

    def member_copy(ref, block, send, recv, i, j):
        slot, source = block_of(ref, i, 0, block)
        return pltpu.make_async_remote_copy(
            src_ref=slot,
            dst_ref=slot,
            send_sem=send.at[i, j - 1],
            recv_sem=recv.at[source],
            device_id=(group * minors + (minor + j) % minors, me_t),
            device_id_type=MESH,
        )

    def arrived(ref, block, recv, i, j):
        slot, source = block_of(ref, i, j, block)
        pltpu.make_async_copy(slot, slot, recv.at[source]).wait()

    first_group = functools.partial(group_copy, first, 2 * windows, first_send, first_recv)
    first_member = functools.partial(member_copy, first, 2 * windows, first_pass, first_recv)
    first_arrived = functools.partial(arrived, first, 2 * windows, first_recv)
    all_group = functools.partial(group_copy, rows_all, held, all_send, all_recv)
    all_member = functools.partial(member_copy, rows_all, held, all_pass, all_recv)
    all_arrived = functools.partial(arrived, rows_all, held, all_recv)

    def spread_copy(s, h, i):
        return pltpu.make_async_remote_copy(
            src_ref=pieces.at[s, h],
            dst_ref=spread.at[s, h, i - 1],
            send_sem=spread_send.at[s, h, i - 1],
            recv_sem=spread_recv.at[s, h, i - 1],
            device_id=((group + i) % nt * minors + minor, me_t),
            device_id_type=MESH,
        )

    def feat_slot(s, h):
        return feats.at[
            s,
            h,
            pl.ds(pl.multiple_of(me_t * rows, rows), rows),
            pl.ds(pl.multiple_of(minor * part, part), part),
        ]

    def feat_copy(s, h, i, j):
        return pltpu.make_async_remote_copy(
            src_ref=pieces.at[s, h] if i == 0 else spread.at[s, h, i - 1],
            dst_ref=feat_slot(s, h),
            send_sem=feat_send.at[s, h, i, j],
            recv_sem=feat_recv.at[s, h, me_t, minor],
            device_id=(group * minors + (minor + j) % minors, (group + nt - i) % nt),
            device_id_type=MESH,
        )

    def feat_local(s, h, i):
        return pltpu.make_async_copy(
            pieces.at[s, h] if i == 0 else spread.at[s, h, i - 1],
            feat_slot(s, h),
            feat_recv.at[s, h, me_t, minor],
        )

    def deliver(s, h, i):
        target = (group + nt - i) % nt
        for j in range(1, minors):
            feat_copy(s, h, i, j).start()

        @pl.when(target != me_t)
        def _():
            feat_copy(s, h, i, 0).start()

        @pl.when(target == me_t)
        def _():
            feat_local(s, h, i).start()

    def launch(s, h):
        for i in order[1:]:
            spread_copy(s, h, i).start()
        deliver(s, h, 0)

    def part_copy(s, n, k):
        return pltpu.make_async_remote_copy(
            src_ref=outgoing.at[s, n, pl.ds(pl.multiple_of((me_t + k) % nt * rows, rows), rows)],
            dst_ref=landed.at[s, n, k - 1],
            send_sem=part_send.at[s, n, k - 1],
            recv_sem=part_recv.at[s, n, k - 1],
            device_id=(me_d, (me_t + k) % nt),
            device_id_type=MESH,
        )

    def share(s, n):
        for k in range(1, nt):
            part_copy(s, n, k).start()

    def summed(s, n):
        total = partial[n, pl.ds(pl.multiple_of(me_t * rows, rows), rows), :]
        for k in range(1, nt):
            part_copy(s, n, k).wait_recv()
            total = total + landed[s, n, k - 1].astype(F32)
        return total

    for i in order[1:]:
        first_group(i).start()
    place = lax.broadcasted_iota(jnp.int32, (held, windows * token_pad), 1)
    row = lax.broadcasted_iota(jnp.int32, (held, windows * token_pad), 0)
    compact = place == row // tokens * token_pad + row % tokens
    rows_all[pl.ds(pl.multiple_of(me_d * held, held), held), :] = jnp.dot(
        jnp.where(compact, 1.0, 0.0).astype(BF16), attended, preferred_element_type=F32
    ).astype(BF16)
    for j in range(1, minors):
        all_member(0, j).start()
    for i in order:
        if i:
            first_arrived(i, 0)
        for j in range(1, minors):
            first_member(i, j).start()
    for i in turns[0]:
        all_group(i).start()
    residual_picked = pick(accepted_ref[:, 0:1], rows, residual_ref[...], tokens)
    load_out.wait()
    for i in order:
        for j in range(1, minors):
            first_arrived(i, j)
    for n in range(CUTS):
        for c in range(0, part, chunk):
            lanes = pl.ds(n * part + c, chunk)
            low = jnp.dot(first[...], out_weight[:half, lanes], preferred_element_type=F32)
            high = jnp.dot(first[...], out_weight[half:, lanes], preferred_element_type=F32)
            product = (
                low.reshape(nd, 2, windows, chunk)[:, 0]
                + high.reshape(nd, 2, windows, chunk)[:, 1]
            ).reshape(nd * windows, chunk)
            partial[n, :, c : c + chunk] = product
            outgoing[STEPS, n, :, c : c + chunk] = product.astype(BF16)
        share(STEPS, n)
    for n in range(CUTS):
        pieces[0, n] = (
            residual_picked[:, n * part : (n + 1) * part] + summed(STEPS, n)
        ).astype(BF16)
        launch(0, n)
    load_draft.wait()

    def rows_copy(i):
        return pltpu.make_async_remote_copy(
            src_ref=rows_out.at[i],
            dst_ref=rows_in.at[me_t],
            send_sem=rows_send.at[i],
            recv_sem=rows_recv.at[me_t],
            device_id=(me_d, (group + nt - i) % nt),
            device_id_type=MESH,
        )

    def project(i):
        for j in range(1, minors):
            all_arrived(i, j)
        target = (group + nt - i) % nt
        span = minors * held
        block = rows_all.at[pl.ds(pl.multiple_of(target * span, span), span)]
        for c in range(0, cols, 256):
            product = jnp.dot(block[...], out_weight[:, c : c + 256], preferred_element_type=F32)
            rows_out[i, :, c : c + 256] = product.astype(BF16)

            @pl.when(target == me_t)
            def _():
                rows_own[:, c : c + 256] = product

        @pl.when(target != me_t)
        def _():
            rows_copy(i).start()

    def forward(i):
        all_arrived(i, 0)
        for j in range(1, minors):
            all_member(i, j).start()

    def collect():
        for k in range(1, nt):
            source = (me_t + k) % nt
            slot = rows_in.at[source]
            pltpu.make_async_copy(slot, slot, rows_recv.at[source]).wait()
        for c in range(0, cols, 256):
            total = rows_own[:, c : c + 256] + residual_ref[:, c : c + 256].astype(F32)
            for k in range(1, nt):
                total = total + rows_in[(me_t + k) % nt, :, c : c + 256].astype(F32)
            verified_ref[:, c : c + 256] = total.astype(BF16)

    def early(s):
        for turn in range(spans + 1):

            @pl.when(s == turn)
            def _(turn=turn):
                for i in turns[turn] if turn < spans else []:
                    forward(i)
                for i in turns[turn - 1] if turn else order[:1]:
                    project(i)

        @pl.when(s == spans + 1)
        def _():
            collect()

    def late(s):
        for turn in range(1, spans):

            @pl.when(s == turn - 1)
            def _(turn=turn):
                for i in turns[turn]:
                    all_group(i).start()

    def step(s, carry):
        early(s)
        for h in range(CUTS):
            for i in order[1:]:
                spread_copy(s, h, i).wait_recv()
                deliver(s, h, i)
        late(s)
        for h in range(CUTS):
            for t in range(nt):
                for m in range(minors):
                    pltpu.make_async_copy(
                        pieces.at[s, h],
                        feats.at[s, h, pl.ds(t * rows, rows), pl.ds(m * part, part)],
                        feat_recv.at[s, h, t, m],
                    ).wait()
            for n in range(CUTS):
                for c in range(0, part, chunk):
                    product = sum(
                        jnp.dot(
                            feats[s, h, :, m * part : (m + 1) * part],
                            draft_weight[
                                pl.ds(m * cols + h * part, part), pl.ds(n * part + c, chunk)
                            ],
                            preferred_element_type=F32,
                        )
                        for m in range(minors)
                    )
                    if h:
                        product = product + partial[n, :, c : c + chunk]
                    partial[n, :, c : c + chunk] = product
                    if h == CUTS - 1:
                        outgoing[s, n, :, c : c + chunk] = product.astype(BF16)
                if h == CUTS - 1:
                    share(s, n)
        for n in range(CUTS):
            drafted = jnp.tanh(2.0 * summed(s, n)).astype(BF16)
            drafted_ref[s, :, n * part : (n + 1) * part] = drafted
            pieces[s + 1, n] = drafted

            @pl.when(s < STEPS - 1)
            def _():
                launch(s + 1, n)

        return carry

    lax.fori_loop(0, STEPS, step, 0)

    def drain(s, carry):
        for h in range(CUTS):
            for i in range(nt):
                if i:
                    spread_copy(s, h, i).wait_send()
                    part_copy(s, h, i).wait_send()
                for j in range(1, minors):
                    feat_copy(s, h, i, j).wait_send()

                @pl.when((group + nt - i) % nt != me_t)
                def _():
                    feat_copy(s, h, i, 0).wait_send()

        return carry

    lax.fori_loop(0, STEPS, drain, 0)
    for i in range(nt):
        if i:
            for n in range(CUTS):
                part_copy(STEPS, n, i).wait_send()
            first_group(i).wait_send()
            all_group(i).wait_send()
        for j in range(1, minors):
            first_member(i, j).wait_send()
            all_member(i, j).wait_send()

        @pl.when((group + nt - i) % nt != me_t)
        def _():
            rows_copy(i).wait_send()

    @pl.when(me_t == group)
    def _():
        for k in range(1, nt):
            accepted_copy(k).wait_send()


def decode(nt, nd, queries, new_keys, new_values, lengths, accepted, residual, *large):
    windows, tokens, depth = queries.shape
    held = windows * tokens
    span, cols = residual.shape
    rows = accepted.shape[0]
    cache, kv_width = large[0].shape[1:]
    token_pad = -(-tokens // 8) * 8
    fresh_pad = -(-tokens // 16) * 16
    minors = nd // nt
    part = cols // CUTS
    dma = pltpu.SemaphoreType.DMA
    vmem = pl.BlockSpec(memory_space=pltpu.VMEM)
    hbm = pl.BlockSpec(memory_space=pltpu.HBM)
    return pl.pallas_call(
        functools.partial(decode_kernel, nt, nd),
        out_shape=(
            jax.ShapeDtypeStruct((span, cols), BF16),
            jax.ShapeDtypeStruct((STEPS, rows, cols), BF16),
        ),
        in_specs=[vmem] * 6 + [hbm] * 4,
        out_specs=(vmem, vmem),
        scratch_shapes=[
            pltpu.VMEM((depth, cols), BF16),
            pltpu.VMEM((depth, cols), BF16),
            pltpu.VMEM((windows, cache + fresh_pad, kv_width), BF16),
            pltpu.VMEM((windows, cache + fresh_pad, kv_width), BF16),
            pltpu.VMEM((windows, token_pad, depth), F32),
            pltpu.VMEM((windows, fresh_pad, kv_width), F32),
            pltpu.VMEM((windows, fresh_pad, kv_width), F32),
            pltpu.VMEM((windows * token_pad, depth), F32),
            pltpu.VMEM(accepted.shape, F32),
            pltpu.VMEM((nd * 2 * windows, depth // 2), BF16),
            pltpu.VMEM((STEPS + 1, CUTS, rows, part), BF16),
            pltpu.VMEM((STEPS, CUTS, nt - 1, rows, part), BF16),
            pltpu.VMEM((STEPS, CUTS, nt * rows, minors * part), BF16),
            pltpu.VMEM((CUTS, nt * rows, part), F32),
            pltpu.VMEM((STEPS + 1, CUTS, nt * rows, part), BF16),
            pltpu.VMEM((STEPS + 1, CUTS, nt - 1, rows, part), BF16),
            pltpu.VMEM((nd * held, depth), BF16),
            pltpu.VMEM((span, cols), F32),
            pltpu.VMEM((nt, span, cols), BF16),
            pltpu.VMEM((nt, span, cols), BF16),
            dma((4,)),
            dma((nt - 1,)),
            dma,
            dma((nt - 1,)),
            dma((nt, minors - 1)),
            dma((nd,)),
            dma((STEPS, CUTS, nt - 1)),
            dma((STEPS, CUTS, nt - 1)),
            dma((STEPS, CUTS, nt, minors)),
            dma((STEPS, CUTS, nt, minors)),
            dma((STEPS + 1, CUTS, nt - 1)),
            dma((STEPS + 1, CUTS, nt - 1)),
            dma((nt - 1,)),
            dma((nt, minors - 1)),
            dma((nd,)),
            dma((nt,)),
            dma((nt,)),
        ],
        compiler_params=pltpu.CompilerParams(
            collective_id=0, has_side_effects=True, vmem_limit_bytes=48 * 1024 * 1024
        ),
        cost_estimate=pl.CostEstimate(
            flops=2 * (STEPS * nt * rows + nd * held) * depth * cols,
            bytes_accessed=4 * depth * cols,
            transcendentals=STEPS * rows * cols,
        ),
    )(queries, new_keys, new_values, lengths, accepted, residual, *large)


def per_device(
    queries,
    new_keys,
    new_values,
    key_cache,
    value_cache,
    cache_lengths,
    accepted,
    residual,
    out_weight,
    draft_weight,
):
    block_windows, block_tokens, block_cols = residual.shape
    verified, drafted = decode(
        lax.axis_size("tensor"),
        lax.axis_size("dp"),
        queries,
        new_keys,
        new_values,
        jnp.broadcast_to(cache_lengths.astype(F32)[:, None], (cache_lengths.shape[0], HD)),
        jnp.broadcast_to(accepted.astype(F32)[:, None], (block_windows, HD)),
        residual.reshape(block_windows * block_tokens, block_cols),
        key_cache,
        value_cache,
        out_weight,
        draft_weight,
    )
    return (verified.reshape(residual.shape), drafted)


def solution(mesh):
    placed = (
        P("dp", None, "tensor"),
        P("dp", None, "tensor"),
        P("dp", None, "tensor"),
        P("dp", None, "tensor"),
        P("dp", None, "tensor"),
        P("dp"),
        P("tensor"),
        P("tensor", None, "dp"),
        P("tensor", "dp"),
        P("tensor", "dp"),
    )
    return jax.shard_map(
        per_device,
        mesh=mesh,
        in_specs=placed,
        out_specs=(P("tensor", None, "dp"), P(None, "tensor", "dp")),
        check_vma=False,
    )
```

```python
import functools

import jax
import jax.numpy as jnp
from jax import lax
from jax.experimental import pallas as pl
from jax.experimental.pallas import tpu as pltpu
from jax.sharding import PartitionSpec as P

HD = 128
STEPS = 5
CUTS = 2


MESH = pl.DeviceIdType.MESH
BF16 = jnp.bfloat16
F32 = jnp.float32


def decode_kernel(
    nt,
    nd,
    queries_ref,
    new_keys_ref,
    new_values_ref,
    lengths_ref,
    accepted_ref,
    residual_ref,
    key_cache_hbm,
    value_cache_hbm,
    out_weight_hbm,
    draft_weight_hbm,
    verified_ref,
    drafted_ref,
    out_weight,
    draft_weight,
    keys,
    values,
    query_pad,
    mixed,
    accepted_near,
    first,
    pieces,
    spread,
    feats,
    partial,
    outgoing,
    landed,
    rows_all,
    rows_own,
    rows_out,
    rows_in,
    weight_sem,
    accepted_send,
    accepted_recv,
    first_send,
    first_pass,
    first_recv,
    spread_send,
    spread_recv,
    feat_send,
    feat_recv,
    part_send,
    part_recv,
    all_send,
    all_pass,
    all_recv,
    rows_send,
    rows_recv,
):
    rows, part = pieces.shape[2:]
    cols = part * CUTS
    chunk = min(part, 256)
    minors = nd // nt
    held, depth = queries_ref.shape
    windows, cache, kv_width = key_cache_hbm.shape
    tokens = held // windows
    slots = keys.shape[1]
    token_pad = mixed.shape[0] // windows
    half = depth // 2
    me_t = lax.axis_index("tensor")
    me_d = lax.axis_index("dp")
    group = me_d // minors
    minor = me_d % minors
    order = sorted(range(nt), key=lambda i: min(i, nt - i))
    spans = max(1, STEPS - 2)
    turns = [
        [i for q, i in enumerate(order[1:]) if q * spans // (nt - 1) == turn]
        for turn in range(spans)
    ]

    load_out = pltpu.make_async_copy(out_weight_hbm, out_weight, weight_sem.at[0])
    load_draft = pltpu.make_async_copy(draft_weight_hbm, draft_weight, weight_sem.at[1])
    load_keys = pltpu.make_async_copy(
        key_cache_hbm, keys.at[:, pl.ds(0, cache)], weight_sem.at[2]
    )
    load_values = pltpu.make_async_copy(
        value_cache_hbm, values.at[:, pl.ds(0, cache)], weight_sem.at[3]
    )
    load_keys.start()
    load_values.start()
    load_out.start()
    load_draft.start()
    barrier = pltpu.get_barrier_semaphore()
    for k in range(nt):
        for j in range(minors):
            if k or j:
                peer = (group * minors + (minor + j) % minors, (me_t + k) % nt)
                pl.semaphore_signal(barrier, inc=1, device_id=peer, device_id_type=MESH)
    for i in range(1, nt):
        peer = ((group + i) % nt * minors + minor, me_t)
        pl.semaphore_signal(barrier, inc=1, device_id=peer, device_id_type=MESH)

    def by_window(table, pad):
        line = lax.broadcasted_iota(jnp.int32, (windows * pad, held), 0)
        place = lax.broadcasted_iota(jnp.int32, (windows * pad, held), 1)
        chosen = (line % pad < tokens) & (place == line % pad * windows + line // pad)
        return jnp.dot(
            jnp.where(chosen, 1.0, 0.0).astype(BF16), table, preferred_element_type=F32
        )

    fresh_pad = slots - cache
    query_pad[...] = by_window(queries_ref[...], token_pad).reshape(query_pad.shape)
    fresh_shape = (windows, fresh_pad, kv_width)
    keys[:, cache:, :] = by_window(new_keys_ref[...], fresh_pad).reshape(fresh_shape).astype(BF16)
    values[:, cache:, :] = (
        by_window(new_values_ref[...], fresh_pad).reshape(fresh_shape).astype(BF16)
    )
    kv_heads = kv_width // HD
    share_heads = depth // kv_width
    query_rows = share_heads * token_pad
    spot = lax.broadcasted_iota(jnp.int32, (query_rows, slots), 1)
    token = lax.broadcasted_iota(jnp.int32, (query_rows, slots), 0) % token_pad
    fresh_live = (spot >= cache) & (spot - cache <= token)

    def attend(chosen_windows):
        units = [(w, k) for w in chosen_windows for k in range(kv_heads)]
        scores = []
        for w, k in units:
            heads = [
                query_pad[w, :, (k * share_heads + h) * HD : (k * share_heads + h + 1) * HD]
                for h in range(share_heads)
            ]
            scores.append(
                lax.dot_general(
                    jnp.concatenate(heads, axis=0).astype(BF16),
                    keys[w, :, k * HD : (k + 1) * HD],
                    (((1,), (1,)), ((), ())),
                    preferred_element_type=F32,
                )
                * HD ** (-0.5)
            )
        weights = []
        for (w, _), score in zip(units, scores):
            cached = (spot < cache) & (spot < lengths_ref[w : w + 1, 0:1])
            score = jnp.where(cached | fresh_live, score, -1e30)
            powered = jnp.exp(score - jnp.max(score, axis=-1, keepdims=True))
            weights.append(
                (powered * (1.0 / jnp.sum(powered, axis=-1, keepdims=True))).astype(BF16)
            )
        for (w, k), weight in zip(units, weights):
            result = jnp.dot(
                weight, values[w, :, k * HD : (k + 1) * HD], preferred_element_type=F32
            )
            for h in range(share_heads):
                head = k * share_heads + h
                mixed[w * token_pad : (w + 1) * token_pad, head * HD : (head + 1) * HD] = result[
                    h * token_pad : (h + 1) * token_pad
                ]

    load_keys.wait()
    load_values.wait()
    attend(range(windows // 2))
    pl.semaphore_wait(barrier, nt * minors - 1 + nt - 1)

    def accepted_copy(k):
        return pltpu.make_async_remote_copy(
            src_ref=accepted_ref,
            dst_ref=accepted_near,
            send_sem=accepted_send.at[k - 1],
            recv_sem=accepted_recv,
            device_id=(me_d, (me_t + k) % nt),
            device_id_type=MESH,
        )

    accepted_local = pltpu.make_async_copy(accepted_ref, accepted_near, accepted_recv)

    @pl.when(me_t == group)
    def _():
        for k in range(1, nt):
            accepted_copy(k).start()
        accepted_local.start()

    attend(range(windows // 2, windows))
    attended = mixed[...].astype(BF16)

    accepted_local.wait()
    near = accepted_near[pl.ds(pl.multiple_of(minor * windows, windows), windows), 0:1]
    window = lax.broadcasted_iota(jnp.int32, (windows, windows * token_pad), 0)
    place = lax.broadcasted_iota(jnp.int32, (windows, windows * token_pad), 1)
    chosen = place == window * token_pad + near - 1
    picked = jnp.dot(
        jnp.where(chosen, 1.0, 0.0).astype(BF16), attended, preferred_element_type=F32
    )
    first[pl.ds(pl.multiple_of(me_d * 2 * windows, 2 * windows), 2 * windows), :] = (
        jnp.concatenate([picked[:, :half], picked[:, half:]], axis=0).astype(BF16)
    )

    def block_of(ref, i, j, block):
        source = (group + nt - i) % nt * minors + (minor + minors - j) % minors
        return ref.at[pl.ds(pl.multiple_of(source * block, block), block)], source

    def group_copy(ref, block, send, recv, i):
        slot, source = block_of(ref, 0, 0, block)
        return pltpu.make_async_remote_copy(
            src_ref=slot,
            dst_ref=slot,
            send_sem=send.at[i - 1],
            recv_sem=recv.at[source],
            device_id=((group + i) % nt * minors + minor, me_t),
            device_id_type=MESH,
        )

    def member_copy(ref, block, send, recv, i, j):
        slot, source = block_of(ref, i, 0, block)
        return pltpu.make_async_remote_copy(
            src_ref=slot,
            dst_ref=slot,
            send_sem=send.at[i, j - 1],
            recv_sem=recv.at[source],
            device_id=(group * minors + (minor + j) % minors, me_t),
            device_id_type=MESH,
        )

    def arrived(ref, block, recv, i, j):
        slot, source = block_of(ref, i, j, block)
        pltpu.make_async_copy(slot, slot, recv.at[source]).wait()

    first_group = functools.partial(group_copy, first, 2 * windows, first_send, first_recv)
    first_member = functools.partial(member_copy, first, 2 * windows, first_pass, first_recv)
    first_arrived = functools.partial(arrived, first, 2 * windows, first_recv)
    all_group = functools.partial(group_copy, rows_all, held, all_send, all_recv)
    all_member = functools.partial(member_copy, rows_all, held, all_pass, all_recv)
    all_arrived = functools.partial(arrived, rows_all, held, all_recv)

    def spread_copy(s, h, i):
        return pltpu.make_async_remote_copy(
            src_ref=pieces.at[s, h],
            dst_ref=spread.at[s, h, i - 1],
            send_sem=spread_send.at[s, h, i - 1],
            recv_sem=spread_recv.at[s, h, i - 1],
            device_id=((group + i) % nt * minors + minor, me_t),
            device_id_type=MESH,
        )

    def feat_slot(s, h):
        return feats.at[
            s,
            h,
            pl.ds(pl.multiple_of(me_t * rows, rows), rows),
            pl.ds(pl.multiple_of(minor * part, part), part),
        ]

    def feat_copy(s, h, i, j):
        return pltpu.make_async_remote_copy(
            src_ref=pieces.at[s, h] if i == 0 else spread.at[s, h, i - 1],
            dst_ref=feat_slot(s, h),
            send_sem=feat_send.at[s, h, i, j],
            recv_sem=feat_recv.at[s, h, me_t, minor],
            device_id=(group * minors + (minor + j) % minors, (group + nt - i) % nt),
            device_id_type=MESH,
        )

    def feat_local(s, h, i):
        return pltpu.make_async_copy(
            pieces.at[s, h] if i == 0 else spread.at[s, h, i - 1],
            feat_slot(s, h),
            feat_recv.at[s, h, me_t, minor],
        )

    def deliver(s, h, i):
        target = (group + nt - i) % nt
        for j in range(1, minors):
            feat_copy(s, h, i, j).start()

        @pl.when(target != me_t)
        def _():
            feat_copy(s, h, i, 0).start()

        @pl.when(target == me_t)
        def _():
            feat_local(s, h, i).start()

    def launch(s, h):
        for i in order[1:]:
            spread_copy(s, h, i).start()
        deliver(s, h, 0)

    def part_copy(s, n, k):
        return pltpu.make_async_remote_copy(
            src_ref=outgoing.at[s, n, pl.ds(pl.multiple_of((me_t + k) % nt * rows, rows), rows)],
            dst_ref=landed.at[s, n, k - 1],
            send_sem=part_send.at[s, n, k - 1],
            recv_sem=part_recv.at[s, n, k - 1],
            device_id=(me_d, (me_t + k) % nt),
            device_id_type=MESH,
        )

    def share(s, n):
        for k in range(1, nt):
            part_copy(s, n, k).start()

    def summed(s, n):
        total = partial[n, pl.ds(pl.multiple_of(me_t * rows, rows), rows), :]
        for k in range(1, nt):
            part_copy(s, n, k).wait_recv()
            total = total + landed[s, n, k - 1].astype(F32)
        return total

    for i in order[1:]:
        first_group(i).start()
    place = lax.broadcasted_iota(jnp.int32, (held, windows * token_pad), 1)
    row = lax.broadcasted_iota(jnp.int32, (held, windows * token_pad), 0)
    compact = place == row % windows * token_pad + row // windows
    rows_all[pl.ds(pl.multiple_of(me_d * held, held), held), :] = jnp.dot(
        jnp.where(compact, 1.0, 0.0).astype(BF16), attended, preferred_element_type=F32
    ).astype(BF16)
    for j in range(1, minors):
        all_member(0, j).start()
    for i in order:
        if i:
            first_arrived(i, 0)
        for j in range(1, minors):
            first_member(i, j).start()
    for i in turns[0]:
        all_group(i).start()
    residual_picked = jnp.zeros((rows, cols), F32)
    for t in range(tokens):
        residual_picked = jnp.where(
            accepted_ref[:, 0:1] == t + 1,
            residual_ref[t * rows : (t + 1) * rows, :].astype(F32),
            residual_picked,
        )
    load_out.wait()
    for i in order:
        for j in range(1, minors):
            first_arrived(i, j)
    for n in range(CUTS):
        for c in range(0, part, chunk):
            lanes = pl.ds(n * part + c, chunk)
            low = jnp.dot(first[...], out_weight[:half, lanes], preferred_element_type=F32)
            high = jnp.dot(first[...], out_weight[half:, lanes], preferred_element_type=F32)
            product = (
                low.reshape(nd, 2, windows, chunk)[:, 0]
                + high.reshape(nd, 2, windows, chunk)[:, 1]
            ).reshape(nd * windows, chunk)
            partial[n, :, c : c + chunk] = product
            outgoing[STEPS, n, :, c : c + chunk] = product.astype(BF16)
        share(STEPS, n)
    for n in range(CUTS):
        pieces[0, n] = (
            residual_picked[:, n * part : (n + 1) * part] + summed(STEPS, n)
        ).astype(BF16)
        launch(0, n)
    load_draft.wait()

    def rows_copy(i):
        return pltpu.make_async_remote_copy(
            src_ref=rows_out.at[i],
            dst_ref=rows_in.at[me_t],
            send_sem=rows_send.at[i],
            recv_sem=rows_recv.at[me_t],
            device_id=(me_d, (group + nt - i) % nt),
            device_id_type=MESH,
        )

    def project(i):
        for j in range(1, minors):
            all_arrived(i, j)
        target = (group + nt - i) % nt
        span = minors * held
        block = rows_all.at[pl.ds(pl.multiple_of(target * span, span), span)]
        for c in range(0, cols, 256):
            product = jnp.dot(block[...], out_weight[:, c : c + 256], preferred_element_type=F32)
            rows_out[i, :, c : c + 256] = product.astype(BF16)

            @pl.when(target == me_t)
            def _():
                rows_own[:, c : c + 256] = product

        @pl.when(target != me_t)
        def _():
            rows_copy(i).start()

    def forward(i):
        all_arrived(i, 0)
        for j in range(1, minors):
            all_member(i, j).start()

    def collect():
        for k in range(1, nt):
            source = (me_t + k) % nt
            slot = rows_in.at[source]
            pltpu.make_async_copy(slot, slot, rows_recv.at[source]).wait()
        for c in range(0, cols, 256):
            total = rows_own[:, c : c + 256]
            for k in range(1, nt):
                total = total + rows_in[(me_t + k) % nt, :, c : c + 256].astype(F32)
            total = total.reshape(minors, tokens, windows, 256)
            for t in range(tokens):
                spot = pl.ds(t * rows, rows)
                verified_ref[spot, c : c + 256] = (
                    total[:, t].reshape(rows, 256) + residual_ref[spot, c : c + 256].astype(F32)
                ).astype(BF16)

    def early(s):
        for turn in range(spans + 1):

            @pl.when(s == turn)
            def _(turn=turn):
                for i in turns[turn] if turn < spans else []:
                    forward(i)
                for i in turns[turn - 1] if turn else order[:1]:
                    project(i)

        @pl.when(s == spans + 1)
        def _():
            collect()

    def late(s):
        for turn in range(1, spans):

            @pl.when(s == turn - 1)
            def _(turn=turn):
                for i in turns[turn]:
                    all_group(i).start()

    def step(s, carry):
        early(s)
        for h in range(CUTS):
            for i in order[1:]:
                spread_copy(s, h, i).wait_recv()
                deliver(s, h, i)
        late(s)
        for h in range(CUTS):
            for t in range(nt):
                for m in range(minors):
                    pltpu.make_async_copy(
                        pieces.at[s, h],
                        feats.at[s, h, pl.ds(t * rows, rows), pl.ds(m * part, part)],
                        feat_recv.at[s, h, t, m],
                    ).wait()
            for n in range(CUTS):
                for c in range(0, part, chunk):
                    product = sum(
                        jnp.dot(
                            feats[s, h, :, m * part : (m + 1) * part],
                            draft_weight[
                                pl.ds(m * cols + h * part, part), pl.ds(n * part + c, chunk)
                            ],
                            preferred_element_type=F32,
                        )
                        for m in range(minors)
                    )
                    if h:
                        product = product + partial[n, :, c : c + chunk]
                    partial[n, :, c : c + chunk] = product
                    if h == CUTS - 1:
                        outgoing[s, n, :, c : c + chunk] = product.astype(BF16)
                if h == CUTS - 1:
                    share(s, n)
        for n in range(CUTS):
            drafted = jnp.tanh(2.0 * summed(s, n)).astype(BF16)
            drafted_ref[s, :, n * part : (n + 1) * part] = drafted
            pieces[s + 1, n] = drafted

            @pl.when(s < STEPS - 1)
            def _():
                launch(s + 1, n)

        return carry

    lax.fori_loop(0, STEPS, step, 0)

    def drain(s, carry):
        for h in range(CUTS):
            for i in range(nt):
                if i:
                    spread_copy(s, h, i).wait_send()
                    part_copy(s, h, i).wait_send()
                for j in range(1, minors):
                    feat_copy(s, h, i, j).wait_send()

                @pl.when((group + nt - i) % nt != me_t)
                def _():
                    feat_copy(s, h, i, 0).wait_send()

        return carry

    lax.fori_loop(0, STEPS, drain, 0)
    for i in range(nt):
        if i:
            for n in range(CUTS):
                part_copy(STEPS, n, i).wait_send()
            first_group(i).wait_send()
            all_group(i).wait_send()
        for j in range(1, minors):
            first_member(i, j).wait_send()
            all_member(i, j).wait_send()

        @pl.when((group + nt - i) % nt != me_t)
        def _():
            rows_copy(i).wait_send()

    @pl.when(me_t == group)
    def _():
        for k in range(1, nt):
            accepted_copy(k).wait_send()


def decode(nt, nd, queries, new_keys, new_values, lengths, accepted, residual, *large):
    held, depth = queries.shape
    span, cols = residual.shape
    rows = accepted.shape[0]
    windows, cache, kv_width = large[0].shape
    tokens = held // windows
    token_pad = -(-tokens // 8) * 8
    fresh_pad = -(-tokens // 16) * 16
    minors = nd // nt
    part = cols // CUTS
    dma = pltpu.SemaphoreType.DMA
    vmem = pl.BlockSpec(memory_space=pltpu.VMEM)
    hbm = pl.BlockSpec(memory_space=pltpu.HBM)
    return pl.pallas_call(
        functools.partial(decode_kernel, nt, nd),
        out_shape=(
            jax.ShapeDtypeStruct((span, cols), BF16),
            jax.ShapeDtypeStruct((STEPS, rows, cols), BF16),
        ),
        in_specs=[vmem] * 6 + [hbm] * 4,
        out_specs=(vmem, vmem),
        scratch_shapes=[
            pltpu.VMEM((depth, cols), BF16),
            pltpu.VMEM((depth, cols), BF16),
            pltpu.VMEM((windows, cache + fresh_pad, kv_width), BF16),
            pltpu.VMEM((windows, cache + fresh_pad, kv_width), BF16),
            pltpu.VMEM((windows, token_pad, depth), F32),
            pltpu.VMEM((windows * token_pad, depth), F32),
            pltpu.VMEM(accepted.shape, jnp.int32),
            pltpu.VMEM((nd * 2 * windows, depth // 2), BF16),
            pltpu.VMEM((STEPS + 1, CUTS, rows, part), BF16),
            pltpu.VMEM((STEPS, CUTS, nt - 1, rows, part), BF16),
            pltpu.VMEM((STEPS, CUTS, nt * rows, minors * part), BF16),
            pltpu.VMEM((CUTS, nt * rows, part), F32),
            pltpu.VMEM((STEPS + 1, CUTS, nt * rows, part), BF16),
            pltpu.VMEM((STEPS + 1, CUTS, nt - 1, rows, part), BF16),
            pltpu.VMEM((nd * held, depth), BF16),
            pltpu.VMEM((span, cols), F32),
            pltpu.VMEM((nt, span, cols), BF16),
            pltpu.VMEM((nt, span, cols), BF16),
            dma((4,)),
            dma((nt - 1,)),
            dma,
            dma((nt - 1,)),
            dma((nt, minors - 1)),
            dma((nd,)),
            dma((STEPS, CUTS, nt - 1)),
            dma((STEPS, CUTS, nt - 1)),
            dma((STEPS, CUTS, nt, minors)),
            dma((STEPS, CUTS, nt, minors)),
            dma((STEPS + 1, CUTS, nt - 1)),
            dma((STEPS + 1, CUTS, nt - 1)),
            dma((nt - 1,)),
            dma((nt, minors - 1)),
            dma((nd,)),
            dma((nt,)),
            dma((nt,)),
        ],
        compiler_params=pltpu.CompilerParams(
            collective_id=0, has_side_effects=True, vmem_limit_bytes=62 * 1024 * 1024
        ),
        cost_estimate=pl.CostEstimate(
            flops=2 * (STEPS * nt * rows + nd * held) * depth * cols,
            bytes_accessed=4 * depth * cols,
            transcendentals=STEPS * rows * cols,
        ),
    )(queries, new_keys, new_values, lengths, accepted, residual, *large)


def per_device(
    queries,
    new_keys,
    new_values,
    key_cache,
    value_cache,
    cache_lengths,
    accepted,
    residual,
    out_weight,
    draft_weight,
):
    def flat(table):
        return jnp.swapaxes(table, 0, 1).reshape(-1, table.shape[2])

    block_windows, block_tokens, block_cols = residual.shape
    verified, drafted = decode(
        lax.axis_size("tensor"),
        lax.axis_size("dp"),
        flat(queries),
        flat(new_keys),
        flat(new_values),
        jnp.broadcast_to(cache_lengths[:, None], (cache_lengths.shape[0], HD)),
        jnp.broadcast_to(accepted[:, None], (block_windows, HD)),
        flat(residual),
        key_cache,
        value_cache,
        out_weight,
        draft_weight,
    )
    verified = verified.reshape(block_tokens, block_windows, block_cols)
    return (jnp.swapaxes(verified, 0, 1), drafted)


def solution(mesh):
    placed = (
        P("dp", None, "tensor"),
        P("dp", None, "tensor"),
        P("dp", None, "tensor"),
        P("dp", None, "tensor"),
        P("dp", None, "tensor"),
        P("dp"),
        P("tensor"),
        P("tensor", None, "dp"),
        P("tensor", "dp"),
        P("tensor", "dp"),
    )
    return jax.shard_map(
        per_device,
        mesh=mesh,
        in_specs=placed,
        out_specs=(P("tensor", None, "dp"), P(None, "tensor", "dp")),
        check_vma=False,
    )
```

```python
import functools

import jax
import jax.numpy as jnp
from jax import lax
from jax.experimental import pallas as pl
from jax.experimental.pallas import tpu as pltpu
from jax.sharding import PartitionSpec as P

HD = 128
STEPS = 5
CUTS = 2


MESH = pl.DeviceIdType.MESH
BF16 = jnp.bfloat16
F32 = jnp.float32


def decode_kernel(
    nt,
    nd,
    queries_ref,
    new_keys_ref,
    new_values_ref,
    lengths_ref,
    accepted_ref,
    residual_ref,
    key_cache_hbm,
    value_cache_hbm,
    out_weight_hbm,
    draft_weight_hbm,
    verified_ref,
    drafted_ref,
    out_weight,
    draft_weight,
    keys,
    values,
    query_pad,
    mixed,
    accepted_near,
    first,
    pieces,
    spread,
    feats,
    partial,
    outgoing,
    landed,
    rows_all,
    rows_own,
    rows_out,
    rows_in,
    weight_sem,
    accepted_send,
    accepted_recv,
    first_send,
    first_pass,
    first_recv,
    spread_send,
    spread_recv,
    feat_send,
    feat_recv,
    part_send,
    part_recv,
    all_send,
    all_pass,
    all_recv,
    rows_send,
    rows_recv,
):
    rows, part = pieces.shape[2:]
    cols = part * CUTS
    chunk = min(part, 256)
    minors = nd // nt
    held, depth = queries_ref.shape
    windows, cache, kv_width = key_cache_hbm.shape
    tokens = held // windows
    slots = keys.shape[1]
    token_pad = mixed.shape[0] // windows
    half = depth // 2
    me_t = lax.axis_index("tensor")
    me_d = lax.axis_index("dp")
    group = me_d // minors
    minor = me_d % minors
    order = sorted(range(nt), key=lambda i: min(i, nt - i))
    spans = max(1, STEPS - 2)
    turns = [
        [i for q, i in enumerate(order[1:]) if q * spans // (nt - 1) == turn]
        for turn in range(spans)
    ]

    load_out = pltpu.make_async_copy(out_weight_hbm, out_weight, weight_sem.at[0])
    load_draft = pltpu.make_async_copy(draft_weight_hbm, draft_weight, weight_sem.at[1])
    load_keys = pltpu.make_async_copy(
        key_cache_hbm, keys.at[:, pl.ds(0, cache)], weight_sem.at[2]
    )
    load_values = pltpu.make_async_copy(
        value_cache_hbm, values.at[:, pl.ds(0, cache)], weight_sem.at[3]
    )
    load_keys.start()
    load_values.start()
    load_out.start()
    load_draft.start()
    barrier = pltpu.get_barrier_semaphore()
    for k in range(nt):
        for j in range(minors):
            if k or j:
                peer = (group * minors + (minor + j) % minors, (me_t + k) % nt)
                pl.semaphore_signal(barrier, inc=1, device_id=peer, device_id_type=MESH)
    for i in range(1, nt):
        peer = ((group + i) % nt * minors + minor, me_t)
        pl.semaphore_signal(barrier, inc=1, device_id=peer, device_id_type=MESH)

    def by_window(table, pad):
        line = lax.broadcasted_iota(jnp.int32, (windows * pad, held), 0)
        place = lax.broadcasted_iota(jnp.int32, (windows * pad, held), 1)
        chosen = (line % pad < tokens) & (place == line % pad * windows + line // pad)
        return jnp.dot(
            jnp.where(chosen, 1.0, 0.0).astype(BF16), table, preferred_element_type=F32
        )

    fresh_pad = slots - cache
    query_pad[...] = by_window(queries_ref[...], token_pad).reshape(query_pad.shape)
    fresh_shape = (windows, fresh_pad, kv_width)
    keys[:, cache:, :] = by_window(new_keys_ref[...], fresh_pad).reshape(fresh_shape).astype(BF16)
    values[:, cache:, :] = (
        by_window(new_values_ref[...], fresh_pad).reshape(fresh_shape).astype(BF16)
    )
    kv_heads = kv_width // HD
    share_heads = depth // kv_width
    query_rows = share_heads * token_pad
    spot = lax.broadcasted_iota(jnp.int32, (query_rows, slots), 1)
    token = lax.broadcasted_iota(jnp.int32, (query_rows, slots), 0) % token_pad
    fresh_live = (spot >= cache) & (spot - cache <= token)

    def attend(chosen_windows):
        units = [(w, k) for w in chosen_windows for k in range(kv_heads)]
        scores = []
        for w, k in units:
            heads = [
                query_pad[w, :, (k * share_heads + h) * HD : (k * share_heads + h + 1) * HD]
                for h in range(share_heads)
            ]
            scores.append(
                lax.dot_general(
                    jnp.concatenate(heads, axis=0).astype(BF16),
                    keys[w, :, k * HD : (k + 1) * HD],
                    (((1,), (1,)), ((), ())),
                    preferred_element_type=F32,
                )
                * HD ** (-0.5)
            )
        weights = []
        for (w, _), score in zip(units, scores):
            cached = (spot < cache) & (spot < lengths_ref[w : w + 1, 0:1])
            score = jnp.where(cached | fresh_live, score, -1e30)
            powered = jnp.exp(score - jnp.max(score, axis=-1, keepdims=True))
            weights.append(
                (powered * (1.0 / jnp.sum(powered, axis=-1, keepdims=True))).astype(BF16)
            )
        for (w, k), weight in zip(units, weights):
            result = jnp.dot(
                weight, values[w, :, k * HD : (k + 1) * HD], preferred_element_type=F32
            )
            for h in range(share_heads):
                head = k * share_heads + h
                mixed[w * token_pad : (w + 1) * token_pad, head * HD : (head + 1) * HD] = result[
                    h * token_pad : (h + 1) * token_pad
                ]

    load_keys.wait()
    load_values.wait()
    attend(range(windows // 2))
    pl.semaphore_wait(barrier, nt * minors - 1 + nt - 1)

    def accepted_copy(k):
        return pltpu.make_async_remote_copy(
            src_ref=accepted_ref,
            dst_ref=accepted_near,
            send_sem=accepted_send.at[k - 1],
            recv_sem=accepted_recv,
            device_id=(me_d, (me_t + k) % nt),
            device_id_type=MESH,
        )

    accepted_local = pltpu.make_async_copy(accepted_ref, accepted_near, accepted_recv)

    @pl.when(me_t == group)
    def _():
        for k in range(1, nt):
            accepted_copy(k).start()
        accepted_local.start()

    attend(range(windows // 2, windows))
    attended = mixed[...].astype(BF16)

    accepted_local.wait()
    near = accepted_near[pl.ds(pl.multiple_of(minor * windows, windows), windows), 0:1]
    window = lax.broadcasted_iota(jnp.int32, (windows, windows * token_pad), 0)
    place = lax.broadcasted_iota(jnp.int32, (windows, windows * token_pad), 1)
    chosen = place == window * token_pad + near - 1
    picked = jnp.dot(
        jnp.where(chosen, 1.0, 0.0).astype(BF16), attended, preferred_element_type=F32
    )
    first[pl.ds(pl.multiple_of(me_d * 2 * windows, 2 * windows), 2 * windows), :] = (
        jnp.concatenate([picked[:, :half], picked[:, half:]], axis=0).astype(BF16)
    )

    def block_of(ref, i, j, block):
        source = (group + nt - i) % nt * minors + (minor + minors - j) % minors
        return ref.at[pl.ds(pl.multiple_of(source * block, block), block)], source

    def group_copy(ref, block, send, recv, i):
        slot, source = block_of(ref, 0, 0, block)
        return pltpu.make_async_remote_copy(
            src_ref=slot,
            dst_ref=slot,
            send_sem=send.at[i - 1],
            recv_sem=recv.at[source],
            device_id=((group + i) % nt * minors + minor, me_t),
            device_id_type=MESH,
        )

    def member_copy(ref, block, send, recv, i, j):
        slot, source = block_of(ref, i, 0, block)
        return pltpu.make_async_remote_copy(
            src_ref=slot,
            dst_ref=slot,
            send_sem=send.at[i, j - 1],
            recv_sem=recv.at[source],
            device_id=(group * minors + (minor + j) % minors, me_t),
            device_id_type=MESH,
        )

    def arrived(ref, block, recv, i, j):
        slot, source = block_of(ref, i, j, block)
        pltpu.make_async_copy(slot, slot, recv.at[source]).wait()

    first_group = functools.partial(group_copy, first, 2 * windows, first_send, first_recv)
    first_member = functools.partial(member_copy, first, 2 * windows, first_pass, first_recv)
    first_arrived = functools.partial(arrived, first, 2 * windows, first_recv)
    all_group = functools.partial(group_copy, rows_all, held, all_send, all_recv)
    all_member = functools.partial(member_copy, rows_all, held, all_pass, all_recv)
    all_arrived = functools.partial(arrived, rows_all, held, all_recv)

    def spread_copy(s, h, i):
        return pltpu.make_async_remote_copy(
            src_ref=pieces.at[s, h],
            dst_ref=spread.at[s, h, i - 1],
            send_sem=spread_send.at[s, h, i - 1],
            recv_sem=spread_recv.at[s, h, i - 1],
            device_id=((group + i) % nt * minors + minor, me_t),
            device_id_type=MESH,
        )

    def feat_slot(s, h):
        return feats.at[
            s,
            h,
            pl.ds(pl.multiple_of(me_t * rows, rows), rows),
            pl.ds(pl.multiple_of(minor * part, part), part),
        ]

    def feat_copy(s, h, i, j):
        return pltpu.make_async_remote_copy(
            src_ref=pieces.at[s, h] if i == 0 else spread.at[s, h, i - 1],
            dst_ref=feat_slot(s, h),
            send_sem=feat_send.at[s, h, i, j],
            recv_sem=feat_recv.at[s, h, me_t, minor],
            device_id=(group * minors + (minor + j) % minors, (group + nt - i) % nt),
            device_id_type=MESH,
        )

    def feat_local(s, h, i):
        return pltpu.make_async_copy(
            pieces.at[s, h] if i == 0 else spread.at[s, h, i - 1],
            feat_slot(s, h),
            feat_recv.at[s, h, me_t, minor],
        )

    def deliver(s, h, i):
        target = (group + nt - i) % nt
        for j in range(1, minors):
            feat_copy(s, h, i, j).start()

        @pl.when(target != me_t)
        def _():
            feat_copy(s, h, i, 0).start()

        @pl.when(target == me_t)
        def _():
            feat_local(s, h, i).start()

    def launch(s, h):
        for i in order[1:]:
            spread_copy(s, h, i).start()
        deliver(s, h, 0)

    def part_copy(s, n, k):
        return pltpu.make_async_remote_copy(
            src_ref=outgoing.at[s, n, pl.ds(pl.multiple_of((me_t + k) % nt * rows, rows), rows)],
            dst_ref=landed.at[s, n, k - 1],
            send_sem=part_send.at[s, n, k - 1],
            recv_sem=part_recv.at[s, n, k - 1],
            device_id=(me_d, (me_t + k) % nt),
            device_id_type=MESH,
        )

    def share(s, n):
        for k in range(1, nt):
            part_copy(s, n, k).start()

    def summed(s, n):
        total = partial[n, pl.ds(pl.multiple_of(me_t * rows, rows), rows), :]
        for k in range(1, nt):
            part_copy(s, n, k).wait_recv()
            total = total + landed[s, n, k - 1].astype(F32)
        return total

    for i in order[1:]:
        first_group(i).start()
    place = lax.broadcasted_iota(jnp.int32, (held, windows * token_pad), 1)
    row = lax.broadcasted_iota(jnp.int32, (held, windows * token_pad), 0)
    compact = place == row % windows * token_pad + row // windows
    rows_all[pl.ds(pl.multiple_of(me_d * held, held), held), :] = jnp.dot(
        jnp.where(compact, 1.0, 0.0).astype(BF16), attended, preferred_element_type=F32
    ).astype(BF16)
    for j in range(1, minors):
        all_member(0, j).start()
    for i in order:
        if i:
            first_arrived(i, 0)
        for j in range(1, minors):
            first_member(i, j).start()
    for i in turns[0]:
        all_group(i).start()
    residual_picked = jnp.zeros((rows, cols), F32)
    for t in range(tokens):
        residual_picked = jnp.where(
            accepted_ref[:, 0:1] == t + 1,
            residual_ref[t * rows : (t + 1) * rows, :].astype(F32),
            residual_picked,
        )
    load_out.wait()
    for i in order:
        for j in range(1, minors):
            first_arrived(i, j)
    for n in range(CUTS):
        for c in range(0, part, chunk):
            lanes = pl.ds(n * part + c, chunk)
            low = jnp.dot(first[...], out_weight[:half, lanes], preferred_element_type=F32)
            high = jnp.dot(first[...], out_weight[half:, lanes], preferred_element_type=F32)
            product = (
                low.reshape(nd, 2, windows, chunk)[:, 0]
                + high.reshape(nd, 2, windows, chunk)[:, 1]
            ).reshape(nd * windows, chunk)
            partial[n, :, c : c + chunk] = product
            outgoing[STEPS, n, :, c : c + chunk] = product.astype(BF16)
        share(STEPS, n)
    for n in range(CUTS):
        pieces[0, n] = (
            residual_picked[:, n * part : (n + 1) * part] + summed(STEPS, n)
        ).astype(BF16)
        launch(0, n)
    load_draft.wait()

    def rows_copy(i):
        return pltpu.make_async_remote_copy(
            src_ref=rows_out.at[i],
            dst_ref=rows_in.at[me_t],
            send_sem=rows_send.at[i],
            recv_sem=rows_recv.at[me_t],
            device_id=(me_d, (group + nt - i) % nt),
            device_id_type=MESH,
        )

    def project(i, n):
        if n == 0:
            for j in range(1, minors):
                all_arrived(i, j)
        target = (group + nt - i) % nt
        span = minors * held
        block = rows_all.at[pl.ds(pl.multiple_of(target * span, span), span)]
        for c in range(n * part, (n + 1) * part, chunk):
            product = jnp.dot(
                block[...], out_weight[:, c : c + chunk], preferred_element_type=F32
            )
            rows_out[i, :, c : c + chunk] = product.astype(BF16)

            @pl.when(target == me_t)
            def _():
                rows_own[:, c : c + chunk] = product

        if n == CUTS - 1:

            @pl.when(target != me_t)
            def _():
                rows_copy(i).start()

    def forward(i):
        all_arrived(i, 0)
        for j in range(1, minors):
            all_member(i, j).start()

    def collect():
        for k in range(1, nt):
            source = (me_t + k) % nt
            slot = rows_in.at[source]
            pltpu.make_async_copy(slot, slot, rows_recv.at[source]).wait()
        for c in range(0, cols, 256):
            total = rows_own[:, c : c + 256]
            for k in range(1, nt):
                total = total + rows_in[(me_t + k) % nt, :, c : c + 256].astype(F32)
            total = total.reshape(minors, tokens, windows, 256)
            for t in range(tokens):
                spot = pl.ds(t * rows, rows)
                verified_ref[spot, c : c + 256] = (
                    total[:, t].reshape(rows, 256) + residual_ref[spot, c : c + 256].astype(F32)
                ).astype(BF16)

    def early(s):
        for turn in range(spans + 1):

            @pl.when(s == turn)
            def _(turn=turn):
                for i in turns[turn] if turn < spans else []:
                    forward(i)
                for i in turns[turn - 1] if turn else order[:1]:
                    project(i, 0)

        @pl.when(s == spans + 1)
        def _():
            collect()

    def late(s):
        for turn in range(spans + 1):

            @pl.when(s == turn)
            def _(turn=turn):
                for i in turns[turn + 1] if turn + 1 < spans else []:
                    all_group(i).start()
                for i in turns[turn - 1] if turn else order[:1]:
                    for n in range(1, CUTS):
                        project(i, n)

    def step(s, carry):
        early(s)
        for h in range(CUTS):
            for i in order[1:]:
                spread_copy(s, h, i).wait_recv()
                deliver(s, h, i)
        late(s)
        for h in range(CUTS):
            for t in range(nt):
                for m in range(minors):
                    pltpu.make_async_copy(
                        pieces.at[s, h],
                        feats.at[s, h, pl.ds(t * rows, rows), pl.ds(m * part, part)],
                        feat_recv.at[s, h, t, m],
                    ).wait()
            for n in range(CUTS):
                for c in range(0, part, chunk):
                    product = sum(
                        jnp.dot(
                            feats[s, h, :, m * part : (m + 1) * part],
                            draft_weight[
                                pl.ds(m * cols + h * part, part), pl.ds(n * part + c, chunk)
                            ],
                            preferred_element_type=F32,
                        )
                        for m in range(minors)
                    )
                    if h:
                        product = product + partial[n, :, c : c + chunk]
                    partial[n, :, c : c + chunk] = product
                    if h == CUTS - 1:
                        outgoing[s, n, :, c : c + chunk] = product.astype(BF16)
                if h == CUTS - 1:
                    share(s, n)
        for n in range(CUTS):
            drafted = jnp.tanh(2.0 * summed(s, n)).astype(BF16)
            drafted_ref[s, :, n * part : (n + 1) * part] = drafted
            pieces[s + 1, n] = drafted

            @pl.when(s < STEPS - 1)
            def _():
                launch(s + 1, n)

        return carry

    lax.fori_loop(0, STEPS, step, 0)

    def drain(s, carry):
        for h in range(CUTS):
            for i in range(nt):
                if i:
                    spread_copy(s, h, i).wait_send()
                    part_copy(s, h, i).wait_send()
                for j in range(1, minors):
                    feat_copy(s, h, i, j).wait_send()

                @pl.when((group + nt - i) % nt != me_t)
                def _():
                    feat_copy(s, h, i, 0).wait_send()

        return carry

    lax.fori_loop(0, STEPS, drain, 0)
    for i in range(nt):
        if i:
            for n in range(CUTS):
                part_copy(STEPS, n, i).wait_send()
            first_group(i).wait_send()
            all_group(i).wait_send()
        for j in range(1, minors):
            first_member(i, j).wait_send()
            all_member(i, j).wait_send()

        @pl.when((group + nt - i) % nt != me_t)
        def _():
            rows_copy(i).wait_send()

    @pl.when(me_t == group)
    def _():
        for k in range(1, nt):
            accepted_copy(k).wait_send()


def decode(nt, nd, queries, new_keys, new_values, lengths, accepted, residual, *large):
    held, depth = queries.shape
    span, cols = residual.shape
    rows = accepted.shape[0]
    windows, cache, kv_width = large[0].shape
    tokens = held // windows
    token_pad = -(-tokens // 8) * 8
    fresh_pad = -(-tokens // 16) * 16
    minors = nd // nt
    part = cols // CUTS
    dma = pltpu.SemaphoreType.DMA
    vmem = pl.BlockSpec(memory_space=pltpu.VMEM)
    hbm = pl.BlockSpec(memory_space=pltpu.HBM)
    return pl.pallas_call(
        functools.partial(decode_kernel, nt, nd),
        out_shape=(
            jax.ShapeDtypeStruct((span, cols), BF16),
            jax.ShapeDtypeStruct((STEPS, rows, cols), BF16),
        ),
        in_specs=[vmem] * 6 + [hbm] * 4,
        out_specs=(vmem, vmem),
        scratch_shapes=[
            pltpu.VMEM((depth, cols), BF16),
            pltpu.VMEM((depth, cols), BF16),
            pltpu.VMEM((windows, cache + fresh_pad, kv_width), BF16),
            pltpu.VMEM((windows, cache + fresh_pad, kv_width), BF16),
            pltpu.VMEM((windows, token_pad, depth), F32),
            pltpu.VMEM((windows * token_pad, depth), F32),
            pltpu.VMEM(accepted.shape, jnp.int32),
            pltpu.VMEM((nd * 2 * windows, depth // 2), BF16),
            pltpu.VMEM((STEPS + 1, CUTS, rows, part), BF16),
            pltpu.VMEM((STEPS, CUTS, nt - 1, rows, part), BF16),
            pltpu.VMEM((STEPS, CUTS, nt * rows, minors * part), BF16),
            pltpu.VMEM((CUTS, nt * rows, part), F32),
            pltpu.VMEM((STEPS + 1, CUTS, nt * rows, part), BF16),
            pltpu.VMEM((STEPS + 1, CUTS, nt - 1, rows, part), BF16),
            pltpu.VMEM((nd * held, depth), BF16),
            pltpu.VMEM((span, cols), F32),
            pltpu.VMEM((nt, span, cols), BF16),
            pltpu.VMEM((nt, span, cols), BF16),
            dma((4,)),
            dma((nt - 1,)),
            dma,
            dma((nt - 1,)),
            dma((nt, minors - 1)),
            dma((nd,)),
            dma((STEPS, CUTS, nt - 1)),
            dma((STEPS, CUTS, nt - 1)),
            dma((STEPS, CUTS, nt, minors)),
            dma((STEPS, CUTS, nt, minors)),
            dma((STEPS + 1, CUTS, nt - 1)),
            dma((STEPS + 1, CUTS, nt - 1)),
            dma((nt - 1,)),
            dma((nt, minors - 1)),
            dma((nd,)),
            dma((nt,)),
            dma((nt,)),
        ],
        compiler_params=pltpu.CompilerParams(
            collective_id=0, has_side_effects=True, vmem_limit_bytes=48 * 1024 * 1024
        ),
        cost_estimate=pl.CostEstimate(
            flops=2 * (STEPS * nt * rows + nd * held) * depth * cols,
            bytes_accessed=4 * depth * cols,
            transcendentals=STEPS * rows * cols,
        ),
    )(queries, new_keys, new_values, lengths, accepted, residual, *large)


def per_device(
    queries,
    new_keys,
    new_values,
    key_cache,
    value_cache,
    cache_lengths,
    accepted,
    residual,
    out_weight,
    draft_weight,
):
    def flat(table):
        return jnp.swapaxes(table, 0, 1).reshape(-1, table.shape[2])

    block_windows, block_tokens, block_cols = residual.shape
    verified, drafted = decode(
        lax.axis_size("tensor"),
        lax.axis_size("dp"),
        flat(queries),
        flat(new_keys),
        flat(new_values),
        jnp.broadcast_to(cache_lengths[:, None], (cache_lengths.shape[0], HD)),
        jnp.broadcast_to(accepted[:, None], (block_windows, HD)),
        flat(residual),
        key_cache,
        value_cache,
        out_weight,
        draft_weight,
    )
    verified = verified.reshape(block_tokens, block_windows, block_cols)
    return (jnp.swapaxes(verified, 0, 1), drafted)


def solution(mesh):
    placed = (
        P("dp", None, "tensor"),
        P("dp", None, "tensor"),
        P("dp", None, "tensor"),
        P("dp", None, "tensor"),
        P("dp", None, "tensor"),
        P("dp"),
        P("tensor"),
        P("tensor", None, "dp"),
        P("tensor", "dp"),
        P("tensor", "dp"),
    )
    return jax.shard_map(
        per_device,
        mesh=mesh,
        in_specs=placed,
        out_specs=(P("tensor", None, "dp"), P(None, "tensor", "dp")),
        check_vma=False,
    )
```

```python
import functools

import jax
import jax.numpy as jnp
from jax import lax
from jax.experimental import pallas as pl
from jax.experimental.pallas import tpu as pltpu
from jax.sharding import PartitionSpec as P

HD = 128
STEPS = 5
CUTS = 2


MESH = pl.DeviceIdType.MESH
BF16 = jnp.bfloat16
F32 = jnp.float32


def decode_kernel(
    nt,
    nd,
    queries_ref,
    new_keys_ref,
    new_values_ref,
    lengths_ref,
    accepted_ref,
    residual_ref,
    key_cache_hbm,
    value_cache_hbm,
    out_weight_hbm,
    draft_weight_hbm,
    verified_ref,
    drafted_ref,
    out_weight,
    draft_weight,
    keys,
    values,
    query_pad,
    mixed,
    accepted_near,
    first,
    pieces,
    spread,
    feats,
    partial,
    outgoing,
    landed,
    rows_all,
    rows_own,
    rows_out,
    rows_in,
    weight_sem,
    accepted_send,
    accepted_recv,
    first_send,
    first_pass,
    first_recv,
    spread_send,
    spread_recv,
    feat_send,
    feat_recv,
    part_send,
    part_recv,
    all_send,
    all_pass,
    all_recv,
    rows_send,
    rows_recv,
):
    rows, part = pieces.shape[2:]
    cols = part * CUTS
    chunk = min(part, 256)
    minors = nd // nt
    held, depth = queries_ref.shape
    windows, cache, kv_width = key_cache_hbm.shape
    tokens = held // windows
    slots = keys.shape[1]
    token_pad = mixed.shape[0] // windows
    half = depth // 2
    me_t = lax.axis_index("tensor")
    me_d = lax.axis_index("dp")
    group = me_d // minors
    minor = me_d % minors
    order = sorted(range(nt), key=lambda i: min(i, nt - i))
    spans = max(1, STEPS - 2)
    turns = [
        [i for q, i in enumerate(order[1:]) if q * spans // (nt - 1) == turn]
        for turn in range(spans)
    ]

    load_out = pltpu.make_async_copy(out_weight_hbm, out_weight, weight_sem.at[0])
    load_draft = pltpu.make_async_copy(draft_weight_hbm, draft_weight, weight_sem.at[1])
    load_keys = pltpu.make_async_copy(
        key_cache_hbm, keys.at[:, pl.ds(0, cache)], weight_sem.at[2]
    )
    load_values = pltpu.make_async_copy(
        value_cache_hbm, values.at[:, pl.ds(0, cache)], weight_sem.at[3]
    )
    load_keys.start()
    load_values.start()
    load_out.start()
    load_draft.start()
    barrier = pltpu.get_barrier_semaphore()
    for k in range(nt):
        for j in range(minors):
            if k or j:
                peer = (group * minors + (minor + j) % minors, (me_t + k) % nt)
                pl.semaphore_signal(barrier, inc=1, device_id=peer, device_id_type=MESH)
    for i in range(1, nt):
        peer = ((group + i) % nt * minors + minor, me_t)
        pl.semaphore_signal(barrier, inc=1, device_id=peer, device_id_type=MESH)

    def by_window(table, pad):
        line = lax.broadcasted_iota(jnp.int32, (windows * pad, held), 0)
        place = lax.broadcasted_iota(jnp.int32, (windows * pad, held), 1)
        chosen = (line % pad < tokens) & (place == line % pad * windows + line // pad)
        return jnp.dot(
            jnp.where(chosen, 1.0, 0.0).astype(BF16), table, preferred_element_type=F32
        )

    fresh_pad = slots - cache
    query_pad[...] = by_window(queries_ref[...], token_pad).reshape(query_pad.shape)
    fresh_shape = (windows, fresh_pad, kv_width)
    keys[:, cache:, :] = by_window(new_keys_ref[...], fresh_pad).reshape(fresh_shape).astype(BF16)
    values[:, cache:, :] = (
        by_window(new_values_ref[...], fresh_pad).reshape(fresh_shape).astype(BF16)
    )
    kv_heads = kv_width // HD
    share_heads = depth // kv_width
    query_rows = share_heads * token_pad
    spot = lax.broadcasted_iota(jnp.int32, (query_rows, slots), 1)
    token = lax.broadcasted_iota(jnp.int32, (query_rows, slots), 0) % token_pad
    fresh_live = (spot >= cache) & (spot - cache <= token)

    def attend(chosen_windows):
        units = [(w, k) for w in chosen_windows for k in range(kv_heads)]
        scores = []
        for w, k in units:
            heads = [
                query_pad[w, :, (k * share_heads + h) * HD : (k * share_heads + h + 1) * HD]
                for h in range(share_heads)
            ]
            scores.append(
                lax.dot_general(
                    jnp.concatenate(heads, axis=0).astype(BF16),
                    keys[w, :, k * HD : (k + 1) * HD],
                    (((1,), (1,)), ((), ())),
                    preferred_element_type=F32,
                )
                * HD ** (-0.5)
            )
        weights = []
        for (w, _), score in zip(units, scores):
            cached = (spot < cache) & (spot < lengths_ref[w : w + 1, 0:1])
            score = jnp.where(cached | fresh_live, score, -1e30)
            powered = jnp.exp(score - jnp.max(score, axis=-1, keepdims=True))
            weights.append(
                (powered * (1.0 / jnp.sum(powered, axis=-1, keepdims=True))).astype(BF16)
            )
        for (w, k), weight in zip(units, weights):
            result = jnp.dot(
                weight, values[w, :, k * HD : (k + 1) * HD], preferred_element_type=F32
            )
            for h in range(share_heads):
                head = k * share_heads + h
                mixed[w * token_pad : (w + 1) * token_pad, head * HD : (head + 1) * HD] = result[
                    h * token_pad : (h + 1) * token_pad
                ]

    load_keys.wait()
    load_values.wait()
    attend(range(windows // 2))
    pl.semaphore_wait(barrier, nt * minors - 1 + nt - 1)

    def accepted_copy(k):
        return pltpu.make_async_remote_copy(
            src_ref=accepted_ref,
            dst_ref=accepted_near,
            send_sem=accepted_send.at[k - 1],
            recv_sem=accepted_recv,
            device_id=(me_d, (me_t + k) % nt),
            device_id_type=MESH,
        )

    accepted_local = pltpu.make_async_copy(accepted_ref, accepted_near, accepted_recv)

    @pl.when(me_t == group)
    def _():
        for k in range(1, nt):
            accepted_copy(k).start()
        accepted_local.start()

    attend(range(windows // 2, windows))
    attended = mixed[...].astype(BF16)

    accepted_local.wait()
    near = accepted_near[pl.ds(pl.multiple_of(minor * windows, windows), windows), 0:1]
    window = lax.broadcasted_iota(jnp.int32, (windows, windows * token_pad), 0)
    place = lax.broadcasted_iota(jnp.int32, (windows, windows * token_pad), 1)
    chosen = place == window * token_pad + near - 1
    picked = jnp.dot(
        jnp.where(chosen, 1.0, 0.0).astype(BF16), attended, preferred_element_type=F32
    )
    first[pl.ds(pl.multiple_of(me_d * 2 * windows, 2 * windows), 2 * windows), :] = (
        jnp.concatenate([picked[:, :half], picked[:, half:]], axis=0).astype(BF16)
    )

    def block_of(ref, i, j, block):
        source = (group + nt - i) % nt * minors + (minor + minors - j) % minors
        return ref.at[pl.ds(pl.multiple_of(source * block, block), block)], source

    def group_copy(ref, block, send, recv, i):
        slot, source = block_of(ref, 0, 0, block)
        return pltpu.make_async_remote_copy(
            src_ref=slot,
            dst_ref=slot,
            send_sem=send.at[i - 1],
            recv_sem=recv.at[source],
            device_id=((group + i) % nt * minors + minor, me_t),
            device_id_type=MESH,
        )

    def member_copy(ref, block, send, recv, i, j):
        slot, source = block_of(ref, i, 0, block)
        return pltpu.make_async_remote_copy(
            src_ref=slot,
            dst_ref=slot,
            send_sem=send.at[i, j - 1],
            recv_sem=recv.at[source],
            device_id=(group * minors + (minor + j) % minors, me_t),
            device_id_type=MESH,
        )

    def arrived(ref, block, recv, i, j):
        slot, source = block_of(ref, i, j, block)
        pltpu.make_async_copy(slot, slot, recv.at[source]).wait()

    first_group = functools.partial(group_copy, first, 2 * windows, first_send, first_recv)
    first_member = functools.partial(member_copy, first, 2 * windows, first_pass, first_recv)
    first_arrived = functools.partial(arrived, first, 2 * windows, first_recv)
    all_group = functools.partial(group_copy, rows_all, held, all_send, all_recv)
    all_member = functools.partial(member_copy, rows_all, held, all_pass, all_recv)
    all_arrived = functools.partial(arrived, rows_all, held, all_recv)

    def spread_copy(s, h, i):
        return pltpu.make_async_remote_copy(
            src_ref=pieces.at[s, h],
            dst_ref=spread.at[s, h, i - 1],
            send_sem=spread_send.at[s, h, i - 1],
            recv_sem=spread_recv.at[s, h, i - 1],
            device_id=((group + i) % nt * minors + minor, me_t),
            device_id_type=MESH,
        )

    def feat_slot(s, h):
        return feats.at[
            s,
            h,
            pl.ds(pl.multiple_of(me_t * rows, rows), rows),
            pl.ds(pl.multiple_of(minor * part, part), part),
        ]

    def feat_copy(s, h, i, j):
        return pltpu.make_async_remote_copy(
            src_ref=pieces.at[s, h] if i == 0 else spread.at[s, h, i - 1],
            dst_ref=feat_slot(s, h),
            send_sem=feat_send.at[s, h, i, j],
            recv_sem=feat_recv.at[s, h, me_t, minor],
            device_id=(group * minors + (minor + j) % minors, (group + nt - i) % nt),
            device_id_type=MESH,
        )

    def feat_local(s, h, i):
        return pltpu.make_async_copy(
            pieces.at[s, h] if i == 0 else spread.at[s, h, i - 1],
            feat_slot(s, h),
            feat_recv.at[s, h, me_t, minor],
        )

    def deliver(s, h, i):
        target = (group + nt - i) % nt
        for j in range(1, minors):
            feat_copy(s, h, i, j).start()

        @pl.when(target != me_t)
        def _():
            feat_copy(s, h, i, 0).start()

        @pl.when(target == me_t)
        def _():
            feat_local(s, h, i).start()

    def launch(s, h):
        for i in order[1:]:
            spread_copy(s, h, i).start()
        deliver(s, h, 0)

    def part_copy(s, n, k):
        return pltpu.make_async_remote_copy(
            src_ref=outgoing.at[s, n, pl.ds(pl.multiple_of((me_t + k) % nt * rows, rows), rows)],
            dst_ref=landed.at[s, n, k - 1],
            send_sem=part_send.at[s, n, k - 1],
            recv_sem=part_recv.at[s, n, k - 1],
            device_id=(me_d, (me_t + k) % nt),
            device_id_type=MESH,
        )

    def share(s, n):
        for k in range(1, nt):
            part_copy(s, n, k).start()

    def summed(s, n):
        total = partial[n, pl.ds(pl.multiple_of(me_t * rows, rows), rows), :]
        for k in range(1, nt):
            part_copy(s, n, k).wait_recv()
            total = total + landed[s, n, k - 1].astype(F32)
        return total

    for i in order[1:]:
        first_group(i).start()
    place = lax.broadcasted_iota(jnp.int32, (held, windows * token_pad), 1)
    row = lax.broadcasted_iota(jnp.int32, (held, windows * token_pad), 0)
    compact = place == row % windows * token_pad + row // windows
    rows_all[pl.ds(pl.multiple_of(me_d * held, held), held), :] = jnp.dot(
        jnp.where(compact, 1.0, 0.0).astype(BF16), attended, preferred_element_type=F32
    ).astype(BF16)
    for j in range(1, minors):
        all_member(0, j).start()
    for i in order:
        if i:
            first_arrived(i, 0)
        for j in range(1, minors):
            first_member(i, j).start()
    for i in turns[0]:
        all_group(i).start()
    residual_picked = jnp.zeros((rows, cols), F32)
    for t in range(tokens):
        residual_picked = jnp.where(
            accepted_ref[:, 0:1] == t + 1,
            residual_ref[t * rows : (t + 1) * rows, :].astype(F32),
            residual_picked,
        )
    load_out.wait()
    for i in order:
        for j in range(1, minors):
            first_arrived(i, j)
    for n in range(CUTS):
        for c in range(0, part, chunk):
            lanes = pl.ds(n * part + c, chunk)
            low = jnp.dot(first[...], out_weight[:half, lanes], preferred_element_type=F32)
            high = jnp.dot(first[...], out_weight[half:, lanes], preferred_element_type=F32)
            product = (
                low.reshape(nd, 2, windows, chunk)[:, 0]
                + high.reshape(nd, 2, windows, chunk)[:, 1]
            ).reshape(nd * windows, chunk)
            partial[n, :, c : c + chunk] = product
            outgoing[STEPS, n, :, c : c + chunk] = product.astype(BF16)
        share(STEPS, n)
    for n in range(CUTS):
        pieces[0, n] = (
            residual_picked[:, n * part : (n + 1) * part] + summed(STEPS, n)
        ).astype(BF16)
        launch(0, n)
    load_draft.wait()

    def rows_copy(i):
        return pltpu.make_async_remote_copy(
            src_ref=rows_out.at[i],
            dst_ref=rows_in.at[me_t],
            send_sem=rows_send.at[i],
            recv_sem=rows_recv.at[me_t],
            device_id=(me_d, (group + nt - i) % nt),
            device_id_type=MESH,
        )

    def project(i, n):
        if n == 0:
            for j in range(1, minors):
                all_arrived(i, j)
        target = (group + nt - i) % nt
        span = minors * held
        block = rows_all.at[pl.ds(pl.multiple_of(target * span, span), span)]
        for c in range(n * part, (n + 1) * part, chunk):
            product = jnp.dot(
                block[...], out_weight[:, c : c + chunk], preferred_element_type=F32
            )
            rows_out[i, :, c : c + chunk] = product.astype(BF16)

            @pl.when(target == me_t)
            def _():
                rows_own[:, c : c + chunk] = product

        if n == CUTS - 1:

            @pl.when(target != me_t)
            def _():
                rows_copy(i).start()

    def forward(i):
        all_arrived(i, 0)
        for j in range(1, minors):
            all_member(i, j).start()

    def collect():
        for k in range(1, nt):
            source = (me_t + k) % nt
            slot = rows_in.at[source]
            pltpu.make_async_copy(slot, slot, rows_recv.at[source]).wait()
        for c in range(0, cols, 256):
            total = rows_own[:, c : c + 256]
            for k in range(1, nt):
                total = total + rows_in[(me_t + k) % nt, :, c : c + 256].astype(F32)
            total = total.reshape(minors, tokens, windows, 256)
            for t in range(tokens):
                spot = pl.ds(t * rows, rows)
                verified_ref[spot, c : c + 256] = (
                    total[:, t].reshape(rows, 256) + residual_ref[spot, c : c + 256].astype(F32)
                ).astype(BF16)

    def early(s):
        for turn in range(spans + 1):

            @pl.when(s == turn)
            def _(turn=turn):
                for i in turns[turn] if turn < spans else []:
                    forward(i)
                for i in turns[turn - 1] if turn else order[:1]:
                    project(i, 0)

        @pl.when(s == spans + 1)
        def _():
            collect()

    def late(s):
        for turn in range(spans + 1):

            @pl.when(s == turn)
            def _(turn=turn):
                for i in turns[turn + 1] if turn + 1 < spans else []:
                    all_group(i).start()
                for i in turns[turn - 1] if turn else order[:1]:
                    for n in range(1, CUTS):
                        project(i, n)

    def step(s, carry):
        early(s)
        for h in range(CUTS):
            for i in order[1:]:
                spread_copy(s, h, i).wait_recv()
                deliver(s, h, i)
        late(s)
        for h in range(CUTS):
            for t in range(nt):
                for m in range(minors):
                    pltpu.make_async_copy(
                        pieces.at[s, h],
                        feats.at[s, h, pl.ds(t * rows, rows), pl.ds(m * part, part)],
                        feat_recv.at[s, h, t, m],
                    ).wait()
            for n in range(CUTS):
                for c in range(0, part, chunk):
                    product = sum(
                        jnp.dot(
                            feats[s, h, :, m * part : (m + 1) * part],
                            draft_weight[
                                pl.ds(m * cols + h * part, part), pl.ds(n * part + c, chunk)
                            ],
                            preferred_element_type=F32,
                        )
                        for m in range(minors)
                    )
                    if h:
                        product = product + partial[n, :, c : c + chunk]
                    partial[n, :, c : c + chunk] = product
                    if h == CUTS - 1:
                        outgoing[s, n, :, c : c + chunk] = product.astype(BF16)
                if h == CUTS - 1:
                    share(s, n)
        for n in range(CUTS):
            drafted = jnp.tanh(2.0 * summed(s, n)).astype(BF16)
            drafted_ref[s, :, n * part : (n + 1) * part] = drafted
            pieces[s + 1, n] = drafted

            @pl.when(s < STEPS - 1)
            def _():
                launch(s + 1, n)

        return carry

    lax.fori_loop(0, STEPS, step, 0)

    def drain(s, carry):
        for h in range(CUTS):
            for i in range(nt):
                if i:
                    spread_copy(s, h, i).wait_send()
                    part_copy(s, h, i).wait_send()
                for j in range(1, minors):
                    feat_copy(s, h, i, j).wait_send()

                @pl.when((group + nt - i) % nt != me_t)
                def _():
                    feat_copy(s, h, i, 0).wait_send()

        return carry

    lax.fori_loop(0, STEPS, drain, 0)
    for i in range(nt):
        if i:
            for n in range(CUTS):
                part_copy(STEPS, n, i).wait_send()
            first_group(i).wait_send()
            all_group(i).wait_send()
        for j in range(1, minors):
            first_member(i, j).wait_send()
            all_member(i, j).wait_send()

        @pl.when((group + nt - i) % nt != me_t)
        def _():
            rows_copy(i).wait_send()

    @pl.when(me_t == group)
    def _():
        for k in range(1, nt):
            accepted_copy(k).wait_send()


def decode(nt, nd, queries, new_keys, new_values, lengths, accepted, residual, *large):
    held, depth = queries.shape
    span, cols = residual.shape
    rows = accepted.shape[0]
    windows, cache, kv_width = large[0].shape
    tokens = held // windows
    token_pad = -(-tokens // 8) * 8
    fresh_pad = -(-tokens // 16) * 16
    minors = nd // nt
    part = cols // CUTS
    dma = pltpu.SemaphoreType.DMA
    vmem = pl.BlockSpec(memory_space=pltpu.VMEM)
    hbm = pl.BlockSpec(memory_space=pltpu.HBM)
    return pl.pallas_call(
        functools.partial(decode_kernel, nt, nd),
        out_shape=(
            jax.ShapeDtypeStruct((span, cols), BF16),
            jax.ShapeDtypeStruct((STEPS, rows, cols), BF16),
        ),
        in_specs=[vmem] * 6 + [hbm] * 4,
        out_specs=(vmem, vmem),
        scratch_shapes=[
            pltpu.VMEM((depth, cols), BF16),
            pltpu.VMEM((depth, cols), BF16),
            pltpu.VMEM((windows, cache + fresh_pad, kv_width), BF16),
            pltpu.VMEM((windows, cache + fresh_pad, kv_width), BF16),
            pltpu.VMEM((windows, token_pad, depth), F32),
            pltpu.VMEM((windows * token_pad, depth), F32),
            pltpu.VMEM(accepted.shape, jnp.int32),
            pltpu.VMEM((nd * 2 * windows, depth // 2), BF16),
            pltpu.VMEM((STEPS + 1, CUTS, rows, part), BF16),
            pltpu.VMEM((STEPS, CUTS, nt - 1, rows, part), BF16),
            pltpu.VMEM((STEPS, CUTS, nt * rows, minors * part), BF16),
            pltpu.VMEM((CUTS, nt * rows, part), F32),
            pltpu.VMEM((STEPS + 1, CUTS, nt * rows, part), BF16),
            pltpu.VMEM((STEPS + 1, CUTS, nt - 1, rows, part), BF16),
            pltpu.VMEM((nd * held, depth), BF16),
            pltpu.VMEM((span, cols), F32),
            pltpu.VMEM((nt, span, cols), BF16),
            pltpu.VMEM((nt, span, cols), BF16),
            dma((4,)),
            dma((nt - 1,)),
            dma,
            dma((nt - 1,)),
            dma((nt, minors - 1)),
            dma((nd,)),
            dma((STEPS, CUTS, nt - 1)),
            dma((STEPS, CUTS, nt - 1)),
            dma((STEPS, CUTS, nt, minors)),
            dma((STEPS, CUTS, nt, minors)),
            dma((STEPS + 1, CUTS, nt - 1)),
            dma((STEPS + 1, CUTS, nt - 1)),
            dma((nt - 1,)),
            dma((nt, minors - 1)),
            dma((nd,)),
            dma((nt,)),
            dma((nt,)),
        ],
        compiler_params=pltpu.CompilerParams(
            collective_id=0, has_side_effects=True, vmem_limit_bytes=62 * 1024 * 1024
        ),
        cost_estimate=pl.CostEstimate(
            flops=2 * (STEPS * nt * rows + nd * held) * depth * cols,
            bytes_accessed=4 * depth * cols,
            transcendentals=STEPS * rows * cols,
        ),
    )(queries, new_keys, new_values, lengths, accepted, residual, *large)


def per_device(
    queries,
    new_keys,
    new_values,
    key_cache,
    value_cache,
    cache_lengths,
    accepted,
    residual,
    out_weight,
    draft_weight,
):
    def flat(table):
        return jnp.swapaxes(table, 0, 1).reshape(-1, table.shape[2])

    block_windows, block_tokens, block_cols = residual.shape
    verified, drafted = decode(
        lax.axis_size("tensor"),
        lax.axis_size("dp"),
        flat(queries),
        flat(new_keys),
        flat(new_values),
        jnp.broadcast_to(cache_lengths[:, None], (cache_lengths.shape[0], HD)),
        jnp.broadcast_to(accepted[:, None], (block_windows, HD)),
        flat(residual),
        key_cache,
        value_cache,
        out_weight,
        draft_weight,
    )
    verified = verified.reshape(block_tokens, block_windows, block_cols)
    return (jnp.swapaxes(verified, 0, 1), drafted)


def solution(mesh):
    placed = (
        P("dp", None, "tensor"),
        P("dp", None, "tensor"),
        P("dp", None, "tensor"),
        P("dp", None, "tensor"),
        P("dp", None, "tensor"),
        P("dp"),
        P("tensor"),
        P("tensor", None, "dp"),
        P("tensor", "dp"),
        P("tensor", "dp"),
    )
    return jax.shard_map(
        per_device,
        mesh=mesh,
        in_specs=placed,
        out_specs=(P("tensor", None, "dp"), P(None, "tensor", "dp")),
        check_vma=False,
    )
```
